128 devices in a mesh: dp: 32 (over y, x, z_hi), tensor: 4 (over z_lo, core).
Axes of the slice: x: 4, y: 4, z: 4 (z_hi: 2, z_lo: 2; z = z_hi * 2 + z_lo), core: 2. Of those that a mesh axis runs over, the one named last changes fastest.
Arguments:
- tokens: bfloat16 [16384, 4096], P('dp', 'tensor'), may hold values from -6 to 6
- out_cot: bfloat16 [16384, 4096], P('dp', 'tensor'), may hold values from -6 to 6
- kept_sections: int32 [64, 2], P('tensor'), may hold values from 0 to 3, as said below
- w_in: bfloat16 [64, 3, 256, 256], P('tensor', None, 'dp'), may hold values from -0.21875 to 0.21875
- w_out: bfloat16 [64, 3, 256, 256], P('tensor', None, 'dp'), may hold values from -0.109375 to 0.109375
Outputs:
- mixed: bfloat16 [16384, 4096], P('dp', 'tensor')
- tokens_grad: bfloat16 [16384, 4096], P('dp', 'tensor')
- w_in_grad: float32 [64, 3, 256, 256], P('tensor', None, 'dp')
- w_out_grad: float32 [64, 3, 256, 256], P('tensor', None, 'dp')
The draws below stay inside these ranges and needn't reach their ends.
Inputs may be any that keep to these rules, and one draw needn't show every extreme that they name: `kept_sections`: each row names 2 different sections.
All inputs are finite; a program needn't handle non-finite values.
Results may differ from the reference program's by a relative error of at most 0.018.
Values may be sent and summed in bfloat16 or wider, within the bound.
A program may use at most 192 MiB of HBM per device.

```python
import jax
import jax.numpy as jnp
from jax import lax

D = 4096
BLK = 256
SECTIONS = 4
KEEP = 2
TOK_DEV = 512
DB = 16
HB = 64
SLOTS = 3
TOKENS = 16384


def draw_kept_sections(key, part):
    scores = jax.random.randint(key, (HB, SECTIONS), 0, 1 << 20) * SECTIONS + jnp.arange(SECTIONS, dtype=jnp.int32)[None, :]
    order = jnp.argsort(scores, axis=1)
    return order[:, :KEEP].astype(jnp.int32)


def block_levels(rng, shape, shards, low, high):
    factor_of, own = 1.0, jax.random.fold_in(rng, 6)
    for axis_at, parts in shards:
        heights = jnp.exp(jax.random.uniform(jax.random.fold_in(own, axis_at), (parts,), jnp.float32, low / len(shards), high / len(shards)))
        factor_of = factor_of * jnp.repeat(heights, shape[axis_at] // parts).reshape([-1 if axis == axis_at else 1 for axis in range(len(shape))])
    return factor_of


def normal_values(rng, extent, width, most, shards=(), kind=jnp.bfloat16):
    result = width * jax.random.normal(rng, extent, jnp.float32)
    if shards:
        result = result * block_levels(rng, extent, shards, -0.22, 0.18)
    return jnp.clip(result, -most, most).astype(kind)


def setup_inputs(seed: int = 0) -> dict:
    splits = jax.random.split(jax.random.key(seed), 6)
    return {
        "tokens": normal_values(splits[0], (TOKENS, D), 1.0, 6.0, ((0, 32), (1, 4))),
        "out_cot": normal_values(splits[1], (TOKENS, D), 1.0, 6.0, ((0, 32), (1, 4))),
        "kept_sections": draw_kept_sections(jax.random.fold_in(splits[5], 71), 0),
        "w_in": normal_values(splits[3], (HB, SLOTS, BLK, BLK), (SLOTS * BLK) ** -0.5, 0.21875, ((0, 4), (2, 32))),
        "w_out": normal_values(splits[4], (HB, SLOTS, BLK, BLK), (12 * BLK) ** -0.5, 0.109375, ((0, 4), (2, 32))),
    }


def gelu_slope(pre):
    cdf = 0.5 * (1.0 + lax.erf(pre * 0.7071067811865476))
    return cdf + pre * jnp.exp(-0.5 * pre * pre) * 0.3989422804014327


def block_columns(kept_sections):
    groups = (jnp.arange(HB, dtype=jnp.int32) // (HB // DB)).astype(jnp.int32)
    section_cols = jnp.bitwise_xor(groups[:, None], jnp.left_shift(jnp.int32(1), kept_sections))
    return jnp.concatenate([groups[:, None], section_cols], axis=1).astype(jnp.int32)


def reference(tokens, out_cot, kept_sections, w_in, w_out):
    cols = block_columns(kept_sections)
    route = (cols[:, :, None] == jnp.arange(DB, dtype=jnp.int32)[None, None, :]).astype(jnp.float32)
    scale = float(TOKENS) ** -0.5
    w_in_f = w_in.astype(jnp.float32)
    w_out_f = w_out.astype(jnp.float32)
    blocks = TOKENS // TOK_DEV

    def one_block(carry, pieces):
        acc_in, acc_out = carry
        x_rows, dy_rows = pieces
        x_blocks = x_rows.reshape(TOK_DEV, DB, BLK)
        dy_blocks = dy_rows.reshape(TOK_DEV, DB, BLK)
        picked = x_blocks[:, cols].astype(jnp.float32)
        dpicked = dy_blocks[:, cols].astype(jnp.float32)
        pre = jnp.einsum("thsi,hsio->tho", picked, w_in_f)
        act = jax.nn.gelu(pre, approximate=False).astype(jnp.bfloat16)
        act_f = act.astype(jnp.float32)
        terms = jnp.einsum("thi,hsio->thso", act_f, w_out_f)
        mixed = jnp.einsum("thso,hsd->tdo", terms, route, precision=lax.Precision.HIGHEST)
        act_grad = jnp.einsum("thso,hsio->thi", dpicked, w_out_f)
        pre_grad = (act_grad * gelu_slope(pre)).astype(jnp.bfloat16)
        pre_grad_f = pre_grad.astype(jnp.float32)
        back = jnp.einsum("tho,hsio->thsi", pre_grad_f, w_in_f)
        x_grad = jnp.einsum("thsi,hsd->tdi", back, route, precision=lax.Precision.HIGHEST)
        part_out = jnp.einsum("thi,thso->hsio", act_f, dpicked) * scale
        part_in = jnp.einsum("thsi,tho->hsio", picked, pre_grad_f) * scale
        part_out = lax.optimization_barrier(part_out.astype(jnp.bfloat16)).astype(jnp.float32)
        part_in = lax.optimization_barrier(part_in.astype(jnp.bfloat16)).astype(jnp.float32)
        outs = (mixed.reshape(TOK_DEV, D).astype(jnp.bfloat16), x_grad.reshape(TOK_DEV, D).astype(jnp.bfloat16))
        return (acc_in + part_in, acc_out + part_out), outs

    zeros = jnp.zeros((HB, SLOTS, BLK, BLK), jnp.float32)
    pieces = (tokens.reshape(blocks, TOK_DEV, D), out_cot.reshape(blocks, TOK_DEV, D))
    (w_in_grad, w_out_grad), (mixed, tokens_grad) = lax.scan(one_block, (zeros, zeros), pieces)
    return mixed.reshape(TOKENS, D), tokens_grad.reshape(TOKENS, D), w_in_grad, w_out_grad
```

```python
import functools

import jax
import jax.numpy as jnp
from jax import lax
from jax.experimental import pallas as pl
from jax.experimental.pallas import tpu as pltpu
from jax.sharding import PartitionSpec as P

MESH = pl.DeviceIdType.MESH
F32, BF16 = jnp.float32, jnp.bfloat16
C = 4
J = 4
NB = 12
BLK = 256
TOK = 512
SIGNS = (1, -1)


def nn(a, b):
    return lax.dot_general(a, b, (((1,), (0,)), ((), ())), preferred_element_type=F32)


def nt(a, b):
    return lax.dot_general(a, b, (((1,), (1,)), ((), ())), preferred_element_type=F32)


def kernel(
    kept,
    tokens,
    out_cot,
    w_in,
    w_out,
    mixed,
    tokens_grad,
    w_in_grad,
    w_out_grad,
    g_in,
    g_out,
    t_in,
    t_out,
    r0,
    r1,
    r2,
    r3,
    zh_recv,
    z_send,
    z_recv,
    xs,
    cs,
    xt,
    acc_m,
    acc_n,
    far_send,
    far_recv,
    act_all,
    pg_all,
    ag_send_sem,
    ag_recv_sem,
    rs_send_sem,
    rs_recv_sem,
    zh_send_sem,
    zh_recv_sem,
    tok_send_sem,
    tok_recv_sem,
    far_send_sem,
    far_recv_sem,
    z_send_sem,
    z_recv_sem,
    local_sem,
):
    dp = lax.axis_index("dp")
    te = lax.axis_index("tensor")
    y, x, zh = dp // 8, (dp // 2) % 4, dp % 2
    scale = float(TOK * 32) ** -0.5

    def at(yy, xx, zz):
        return {"dp": (yy % 4) * 8 + (xx % 4) * 2 + zz}

    def beside(axis, d):
        return at(y, x + d + 4, zh) if axis == 0 else at(y + d + 4, x, zh)

    across = {"dp": dp + 1 - 2 * zh}
    core_peer = {"tensor": te + 1 - 2 * (te % 2)}
    z_peer = {"tensor": (te + 2) % 4}
    peers = (core_peer, z_peer)

    def remote(src, dst, send, recv, to):
        return pltpu.make_async_remote_copy(
            src_ref=src, dst_ref=dst, send_sem=send, recv_sem=recv, device_id=to, device_id_type=MESH
        )

    def load(kind, i):
        src, dst = ((tokens, xs), (out_cot, cs))[kind]
        return pltpu.make_async_copy(
            src.at[:, pl.ds(BLK * i, BLK)], dst.at[i], local_sem.at[kind, i]
        )

    for kind in range(2):
        for i in range(C):
            load(kind, i).start()

    barrier = pltpu.get_barrier_semaphore()
    everyone = [across, core_peer, z_peer] + [beside(a, d) for a in (0, 1) for d in SIGNS]
    for to in everyone:
        pl.semaphore_signal(barrier, inc=1, device_id=to, device_id_type=MESH)
    pl.semaphore_wait(barrier, len(everyone))

    def zh_copy(a):
        return remote(
            (w_in, w_out)[a], zh_recv.at[a], zh_send_sem.at[a], zh_recv_sem.at[a], across
        )

    for a in range(2):
        zh_copy(a).start()

    def tok_copy(kind, p, i):
        buf = (xs, cs)[kind]
        return remote(
            buf.at[i],
            buf.at[C * (p + 1) + i],
            tok_send_sem.at[kind, p, i],
            tok_recv_sem.at[kind, p, i],
            peers[p],
        )

    for kind in range(2):
        for i in range(C):
            load(kind, i).wait()

    for a in range(2):
        zh_copy(a).wait_recv()
        own = (w_in, w_out)[a][...].astype(F32).reshape(C, NB, 8, BLK)
        got = zh_recv[a].astype(F32).reshape(C, NB, 8, BLK)
        low = jnp.where(zh == 0, own, got)
        high = jnp.where(zh == 0, got, own)
        piece = jnp.concatenate([low, high], axis=2).astype(BF16)
        (g_in, g_out)[a][:, y, x] = piece

    def opposite(v, d):
        return (v - d + 4) % 4

    def half(d, n):
        return pl.ds(0, n // 2) if d == 1 else pl.ds(n // 2, n // 2)

    def ag_copy(a, c, stage, k):
        d = SIGNS[k]
        g = (g_in, g_out)[a].at[c]
        if stage == 0:
            ref, axis = g.at[y, x], a
        elif stage == 1:
            ref = (g.at[y, opposite(x, d)] if a == 0 else g.at[opposite(y, d), x]).at[half(d, NB)]
            axis = a
        elif stage == 2:
            ref, axis = (g.at[y] if a == 0 else g.at[:, x]), 1 - a
        else:
            ref = g.at[opposite(y, d), half(d, 4)] if a == 0 else g.at[half(d, 4), opposite(x, d)]
            axis = 1 - a
        return remote(
            ref, ref, ag_send_sem.at[a, c, stage, k], ag_recv_sem.at[a, c, stage, k], beside(axis, d)
        )

    def each(fn):
        for a in range(2):
            for k in range(2):
                fn(a, k)

    @pl.loop(0, C)
    def _(c):
        each(lambda a, k: ag_copy(a, c, 0, k).start())

    @pl.loop(0, C)
    def _(i):
        for kind in range(2):
            for p in range(2):
                tok_copy(kind, p, i).start()

    def transpose(i):
        xt[i] = xs[i].T

    @pl.loop(0, C)
    def _(i):
        transpose(i)

    @pl.loop(0, C)
    def _(c):
        def go(a, k):
            ag_copy(a, c, 0, k).wait_recv()
            ag_copy(a, c, 1, k).start()

        each(go)

    @pl.loop(0, C + 1)
    def _(c):
        @pl.when(c < C)
        def _():
            each(lambda a, k: ag_copy(a, c, 1, k).wait_recv())
            each(lambda a, k: ag_copy(a, c, 2, k).start())

        @pl.when(c >= 1)
        def _():
            def go(a, k):
                ag_copy(a, c - 1, 2, k).wait_recv()
                ag_copy(a, c - 1, 3, k).start()

            each(go)

    @pl.loop(0, C)
    def _(i):
        for kind in range(2):
            for p in range(2):
                tok_copy(kind, p, i).wait_recv()

    @pl.loop(C, 3 * C)
    def _(i):
        transpose(i)

    acc_m[...] = jnp.zeros_like(acc_m)
    acc_n[...] = jnp.zeros_like(acc_n)

    def rs_copy(a, c, stage, k):
        d = SIGNS[k]
        t = (t_in, t_out)[a].at[c]
        if stage == 0:
            src = t.at[(y + 2) % 4, half(d, 4)] if a == 0 else t.at[half(d, 4), (x + 2) % 4]
            dst, axis = r0, 1 - a
        elif stage == 1:
            src = t.at[(y + d + 4) % 4] if a == 0 else t.at[:, (x + d + 4) % 4]
            dst, axis = r1, 1 - a
        elif stage == 2:
            src = (t.at[y, (x + 2) % 4] if a == 0 else t.at[(y + 2) % 4, x]).at[half(d, NB)]
            dst, axis = r2, a
        else:
            src = t.at[y, (x + d + 4) % 4] if a == 0 else t.at[(y + d + 4) % 4, x]
            dst, axis = r3, a
        return remote(
            src,
            dst.at[a, c, k],
            rs_send_sem.at[a, c, stage, k],
            rs_recv_sem.at[a, c, stage, k],
            beside(axis, d),
        )

    def add(p, q):
        return p.astype(F32) + q.astype(F32)

    def rs_start(c):
        each(lambda a, k: rs_copy(a, c, 0, k).start())

    def rs_one(c):
        def go(a, k):
            d = SIGNS[k]
            rs_copy(a, c, 0, k).wait_recv()
            if a == 0:
                yy = (y + d + 4) % 4
                t_in[c, yy, half(d, 4)] = add(t_in[c, yy, half(d, 4)], r0[a, c, k]).astype(BF16)
            else:
                xx = (x + d + 4) % 4
                t_out[c, half(d, 4), xx] = add(t_out[c, half(d, 4), xx], r0[a, c, k]).astype(BF16)
            rs_copy(a, c, 1, k).start()

        each(go)

    def rs_two(c):
        for a in range(2):
            for k in range(2):
                rs_copy(a, c, 1, k).wait_recv()
            got = add(r1[a, c, 0], r1[a, c, 1])
            if a == 0:
                t_in[c, y] = (t_in[c, y].astype(F32) + got).astype(BF16)
            else:
                t_out[c, :, x] = (t_out[c, :, x].astype(F32) + got).astype(BF16)
            for k in range(2):
                rs_copy(a, c, 2, k).start()

    def rs_three(c):
        def go(a, k):
            d = SIGNS[k]
            rs_copy(a, c, 2, k).wait_recv()
            if a == 0:
                xx = (x + d + 4) % 4
                t_in[c, y, xx, half(d, NB)] = add(t_in[c, y, xx, half(d, NB)], r2[a, c, k]).astype(BF16)
            else:
                yy = (y + d + 4) % 4
                t_out[c, yy, x, half(d, NB)] = add(t_out[c, yy, x, half(d, NB)], r2[a, c, k]).astype(BF16)
            rs_copy(a, c, 3, k).start()

        each(go)

    def z_copy(a, c):
        return remote(
            z_send.at[a, c], z_recv.at[a, c], z_send_sem.at[a, c], z_recv_sem.at[a, c], across
        )

    def rs_four(c):
        for a in range(2):
            for k in range(2):
                rs_copy(a, c, 3, k).wait_recv()
            total = add(r3[a, c, 0], r3[a, c, 1]) + (t_in, t_out)[a][c, y, x].astype(F32)
            low, high = total[:, :8], total[:, 8:]
            mine = jnp.where(zh == 0, low, high)
            other = jnp.where(zh == 0, high, low)
            z_send[a, c] = other.reshape(NB * 8, BLK).astype(BF16)
            (w_in_grad, w_out_grad)[a][c] = mine
            z_copy(a, c).start()

    def rs_last(c):
        for a in range(2):
            z_copy(a, c).wait_recv()
            out = (w_in_grad, w_out_grad)[a]
            out[c] = out[c] + z_recv[a, c].astype(F32).reshape(NB, 8, BLK)

    def place(section, g):
        near = jnp.where(section == 0, g + 1 - 2 * (g % 2), (g + 2) % 4)
        far = jnp.where(section == 2, C + g, 2 * C + g)
        return jnp.where(section < 2, near, far)

    def block(ref, g, b):
        return ref[g, :, :, b].reshape(BLK, BLK)

    def part_one(g, j):
        h = J * g + j
        ids = [g, place(kept[h, 0], g), place(kept[h, 1], g)]
        ws = [block(g_in, g, 3 * j + s) for s in range(3)]
        pre = nn(xs[ids[0]], ws[0]) + nn(xs[ids[1]], ws[1]) + nn(xs[ids[2]], ws[2])
        cdf = 0.5 * (1.0 + lax.erf(pre * 0.7071067811865476))
        act = (pre * cdf).astype(BF16)
        slope = cdf + pre * jnp.exp(-0.5 * pre * pre) * 0.3989422804014327
        vs = [block(g_out, g, 3 * j + s) for s in range(3)]
        act_grad = nt(cs[ids[0]], vs[0]) + nt(cs[ids[1]], vs[1]) + nt(cs[ids[2]], vs[2])
        pg = (act_grad * slope).astype(BF16)
        act_all[j] = act
        pg_all[j] = pg
        act_t = act.T
        for s in range(3):
            out_term = (nn(act_t, cs[ids[s]]) * scale).astype(BF16)
            t_out[g, :, :, 3 * j + s] = out_term.reshape(4, 4, 16, BLK)
            in_term = (nn(xt[ids[s]], pg) * scale).astype(BF16)
            t_in[g, :, :, 3 * j + s] = in_term.reshape(4, 4, 16, BLK)

    def far_copy(kind, p, g):
        return remote(
            far_send.at[kind, p, g],
            far_recv.at[kind, p, g],
            far_send_sem.at[kind, p, g],
            far_recv_sem.at[kind, p, g],
            peers[p],
        )

    def part_two(g):
        def pick(ref, section):
            def one(j):
                h = J * g + j
                parts = []
                for s in range(2):
                    flag = jnp.where(kept[h, s] == section, 1.0, 0.0).astype(F32)
                    parts.append(block(ref, g, 3 * j + 1 + s).astype(F32) * flag)
                return (parts[0] + parts[1]).astype(BF16)

            return [one(j) for j in range(J)]

        def own(ref):
            return [block(ref, g, 3 * j) for j in range(J)]

        def total(kind, ws):
            if kind == 0:
                act = jnp.concatenate([act_all[j] for j in range(J)], axis=1)
                return nn(act, jnp.concatenate(ws, axis=0))
            pg = jnp.concatenate([pg_all[j] for j in range(J)], axis=1)
            return nt(pg, jnp.concatenate(ws, axis=1))

        for kind in range(2):
            ref = (g_out, g_in)[kind]
            acc = (acc_m, acc_n)[kind]
            for p in range(2):
                far_send[kind, p, g] = total(kind, pick(ref, 2 + p)).astype(BF16)
                far_copy(kind, p, g).start()
            acc[g] = acc[g] + total(kind, own(ref))
            near = (g + 1 - 2 * (g % 2), (g + 2) % 4)
            for p in range(2):
                acc[near[p]] = acc[near[p]] + total(kind, pick(ref, p))

    def wait_gather(c):
        each(lambda a, k: ag_copy(a, c, 3, k).wait_recv())

    @pl.loop(0, C + 3)
    def _(g):
        @pl.when(g < C)
        def _():
            wait_gather(g)

        def halfway(lo):
            @pl.when(g < C)
            def _():
                @pl.loop(lo, lo + 2)
                def _(j):
                    part_one(g, j)

        halfway(0)

        @pl.when((g >= 1) & (g < C + 1))
        def _():
            rs_one(g - 1)

        @pl.when((g >= 2) & (g < C + 2))
        def _():
            rs_three(g - 2)

        halfway(2)

        @pl.when(g < C)
        def _():
            part_two(g)

        @pl.when((g >= 1) & (g < C + 1))
        def _():
            rs_two(g - 1)

        @pl.when((g >= 2) & (g < C + 2))
        def _():
            rs_four(g - 2)

        @pl.when(g < C)
        def _():
            rs_start(g)

        @pl.when(g >= 3)
        def _():
            rs_last(g - 3)

    for kind in range(2):
        stage = (act_all, pg_all)[kind]
        out = (mixed, tokens_grad)[kind]
        for g in range(C):
            for p in range(2):
                far_copy(kind, p, g).wait_recv()
            value = (acc_m, acc_n)[kind][g] + add(far_recv[kind, 0, g], far_recv[kind, 1, g])
            stage[g] = value.astype(BF16)
            pltpu.make_async_copy(
                stage.at[g], out.at[:, pl.ds(BLK * g, BLK)], local_sem.at[kind, g]
            ).start()
    for kind in range(2):
        stage = (act_all, pg_all)[kind]
        out = (mixed, tokens_grad)[kind]
        for g in range(C):
            pltpu.make_async_copy(
                stage.at[g], out.at[:, pl.ds(BLK * g, BLK)], local_sem.at[kind, g]
            ).wait()

    for a in range(2):
        zh_copy(a).wait_send()

    @pl.loop(0, C)
    def _(c):
        for stage in range(4):
            each(lambda a, k: ag_copy(a, c, stage, k).wait_send())
            each(lambda a, k: rs_copy(a, c, stage, k).wait_send())
        for a in range(2):
            z_copy(a, c).wait_send()
            for p in range(2):
                tok_copy(a, p, c).wait_send()
                far_copy(a, p, c).wait_send()


def per_device(tokens, out_cot, kept, w_in, w_out):
    vmem = pl.BlockSpec(memory_space=pltpu.VMEM)
    hbm = pl.BlockSpec(memory_space=pl.ANY)
    dma = pltpu.SemaphoreType.DMA
    full = pltpu.VMEM((C, 4, 4, NB, 16, BLK), BF16)
    row = (TOK, BLK)
    mixed, tokens_grad, w_in_grad, w_out_grad = pl.pallas_call(
        kernel,
        out_shape=(
            jax.ShapeDtypeStruct(tokens.shape, BF16),
            jax.ShapeDtypeStruct(tokens.shape, BF16),
            jax.ShapeDtypeStruct((C, NB, 8, BLK), F32),
            jax.ShapeDtypeStruct((C, NB, 8, BLK), F32),
        ),
        in_specs=[pl.BlockSpec(memory_space=pltpu.SMEM), hbm, hbm, vmem, vmem],
        out_specs=(hbm, hbm, vmem, vmem),
        scratch_shapes=[
            full,
            full,
            full,
            full,
            pltpu.VMEM((2, C, 2, 2, NB, 16, BLK), BF16),
            pltpu.VMEM((2, C, 2, 4, NB, 16, BLK), BF16),
            pltpu.VMEM((2, C, 2, NB // 2, 16, BLK), BF16),
            pltpu.VMEM((2, C, 2, NB, 16, BLK), BF16),
            pltpu.VMEM((2, C * NB * 8, BLK), BF16),
            pltpu.VMEM((2, C, NB * 8, BLK), BF16),
            pltpu.VMEM((2, C, NB * 8, BLK), BF16),
            pltpu.VMEM((3 * C,) + row, BF16),
            pltpu.VMEM((3 * C,) + row, BF16),
            pltpu.VMEM((3 * C, BLK, TOK), BF16),
            pltpu.VMEM((C,) + row, F32),
            pltpu.VMEM((C,) + row, F32),
            pltpu.VMEM((2, 2, C) + row, BF16),
            pltpu.VMEM((2, 2, C) + row, BF16),
            pltpu.VMEM((J,) + row, BF16),
            pltpu.VMEM((J,) + row, BF16),
            dma((2, C, 4, 2)),
            dma((2, C, 4, 2)),
            dma((2, C, 4, 2)),
            dma((2, C, 4, 2)),
            dma((2,)),
            dma((2,)),
            dma((2, 2, C)),
            dma((2, 2, C)),
            dma((2, 2, C)),
            dma((2, 2, C)),
            dma((2, C)),
            dma((2, C)),
            dma((2, C)),
        ],
        compiler_params=pltpu.CompilerParams(
            collective_id=0, has_side_effects=True, vmem_limit_bytes=64 * 2**20
        ),
        cost_estimate=pl.CostEstimate(
            flops=24 * 10**9, bytes_accessed=8 * 2**20, transcendentals=4 * 2**20
        ),
    )(kept, tokens, out_cot, w_in.reshape(C * NB * 8, BLK), w_out.reshape(C * NB * 8, BLK))
    shape = w_in.shape
    return mixed, tokens_grad, w_in_grad.reshape(shape), w_out_grad.reshape(shape)


def solution(mesh):
    wide, blocks = P("dp", "tensor"), P("tensor", None, "dp", None)
    return jax.shard_map(
        per_device,
        mesh=mesh,
        in_specs=(wide, wide, P("tensor", None), blocks, blocks),
        out_specs=(wide, wide, blocks, blocks),
        check_vma=False,
    )
```

```python
import functools

import jax
import jax.numpy as jnp
from jax import lax
from jax.experimental import pallas as pl
from jax.experimental.pallas import tpu as pltpu
from jax.sharding import PartitionSpec as P

MESH = pl.DeviceIdType.MESH
F32, BF16 = jnp.float32, jnp.bfloat16
C = 4
J = 4
NB = 12
BLK = 256
TOK = 512
SIGNS = (1, -1)


def nn(a, b):
    return lax.dot_general(a, b, (((1,), (0,)), ((), ())), preferred_element_type=F32)


def nt(a, b):
    return lax.dot_general(a, b, (((1,), (1,)), ((), ())), preferred_element_type=F32)


def kernel(
    kept,
    tokens,
    out_cot,
    w_in,
    w_out,
    mixed,
    tokens_grad,
    w_in_grad,
    w_out_grad,
    g_in,
    g_out,
    t_in,
    t_out,
    r0,
    r1,
    r2,
    r3,
    zh_recv,
    z_send,
    z_recv,
    xs,
    cs,
    xt,
    acc_m,
    acc_n,
    far_send,
    far_recv,
    act_all,
    pg_all,
    ag_send_sem,
    ag_recv_sem,
    rs_send_sem,
    rs_recv_sem,
    zh_send_sem,
    zh_recv_sem,
    tok_send_sem,
    tok_recv_sem,
    far_send_sem,
    far_recv_sem,
    z_send_sem,
    z_recv_sem,
    local_sem,
):
    dp = lax.axis_index("dp")
    te = lax.axis_index("tensor")
    y, x, zh = dp // 8, (dp // 2) % 4, dp % 2
    scale = float(TOK * 32) ** -0.5

    def at(yy, xx, zz):
        return {"dp": (yy % 4) * 8 + (xx % 4) * 2 + zz}

    def beside(axis, d):
        return at(y, x + d + 4, zh) if axis == 0 else at(y + d + 4, x, zh)

    across = {"dp": dp + 1 - 2 * zh}
    core_peer = {"tensor": te + 1 - 2 * (te % 2)}
    z_peer = {"tensor": (te + 2) % 4}
    peers = (core_peer, z_peer)

    def remote(src, dst, send, recv, to):
        return pltpu.make_async_remote_copy(
            src_ref=src, dst_ref=dst, send_sem=send, recv_sem=recv, device_id=to, device_id_type=MESH
        )

    def load(kind, i):
        src, dst = ((tokens, xs), (out_cot, cs))[kind]
        return pltpu.make_async_copy(
            src.at[:, pl.ds(BLK * i, BLK)], dst.at[i], local_sem.at[kind, i]
        )

    for kind in range(2):
        for i in range(C):
            load(kind, i).start()

    barrier = pltpu.get_barrier_semaphore()
    everyone = [across, core_peer, z_peer] + [beside(a, d) for a in (0, 1) for d in SIGNS]
    for to in everyone:
        pl.semaphore_signal(barrier, inc=1, device_id=to, device_id_type=MESH)
    pl.semaphore_wait(barrier, len(everyone))

    def zh_copy(a, c):
        rows = pl.ds(c * NB * 8, NB * 8)
        return remote(
            (w_in, w_out)[a].at[rows],
            zh_recv.at[a, rows],
            zh_send_sem.at[a, c],
            zh_recv_sem.at[a, c],
            across,
        )

    for c in range(C):
        for a in range(2):
            zh_copy(a, c).start()

    def tok_copy(kind, p, i):
        buf = (xs, cs)[kind]
        return remote(
            buf.at[i],
            buf.at[C * (p + 1) + i],
            tok_send_sem.at[kind, p, i],
            tok_recv_sem.at[kind, p, i],
            peers[p],
        )

    for kind in range(2):
        for i in range(C):
            load(kind, i).wait()

    def join(a, c):
        rows = pl.ds(c * NB * 8, NB * 8)
        zh_copy(a, c).wait_recv()
        own = (w_in, w_out)[a][rows].astype(F32).reshape(NB, 8, BLK)
        got = zh_recv[a, rows].astype(F32).reshape(NB, 8, BLK)
        low = jnp.where(zh == 0, own, got)
        high = jnp.where(zh == 0, got, own)
        (g_in, g_out)[a][c, y, x] = jnp.concatenate([low, high], axis=1).astype(BF16)

    def opposite(v, d):
        return (v - d + 4) % 4

    def half(d, n):
        return pl.ds(0, n // 2) if d == 1 else pl.ds(n // 2, n // 2)

    def ag_copy(a, c, stage, k):
        d = SIGNS[k]
        g = (g_in, g_out)[a].at[c]
        if stage == 0:
            ref, axis = g.at[y, x], a
        elif stage == 1:
            ref = (g.at[y, opposite(x, d)] if a == 0 else g.at[opposite(y, d), x]).at[half(d, NB)]
            axis = a
        elif stage == 2:
            ref, axis = (g.at[y] if a == 0 else g.at[:, x]), 1 - a
        else:
            ref = g.at[opposite(y, d), half(d, 4)] if a == 0 else g.at[half(d, 4), opposite(x, d)]
            axis = 1 - a
        return remote(
            ref, ref, ag_send_sem.at[a, c, stage, k], ag_recv_sem.at[a, c, stage, k], beside(axis, d)
        )

    def each(fn):
        for a in range(2):
            for k in range(2):
                fn(a, k)

    @pl.loop(0, C)
    def _(c):
        for a in range(2):
            join(a, c)
            for k in range(2):
                ag_copy(a, c, 0, k).start()
        for kind in range(2):
            for p in range(2):
                tok_copy(kind, p, c).start()

    def transpose(i):
        xt[i] = xs[i].T

    @pl.loop(0, C)
    def _(i):
        transpose(i)

    @pl.loop(0, C)
    def _(c):
        def go(a, k):
            ag_copy(a, c, 0, k).wait_recv()
            ag_copy(a, c, 1, k).start()

        each(go)

    def ag_three(c):
        def go(a, k):
            ag_copy(a, c, 2, k).wait_recv()
            ag_copy(a, c, 3, k).start()

        each(go)

    @pl.loop(0, C)
    def _(c):
        each(lambda a, k: ag_copy(a, c, 1, k).wait_recv())
        each(lambda a, k: ag_copy(a, c, 2, k).start())

        @pl.when(c >= 1)
        def _():
            ag_three(c - 1)

    @pl.loop(0, C)
    def _(i):
        for kind in range(2):
            for p in range(2):
                tok_copy(kind, p, i).wait_recv()

    @pl.loop(C, 3 * C)
    def _(i):
        transpose(i)

    acc_m[...] = jnp.zeros_like(acc_m)
    acc_n[...] = jnp.zeros_like(acc_n)

    def rs_copy(a, c, stage, k):
        d = SIGNS[k]
        t = (t_in, t_out)[a].at[c]
        if stage == 0:
            src = t.at[(y + 2) % 4, half(d, 4)] if a == 0 else t.at[half(d, 4), (x + 2) % 4]
            dst, axis = r0, 1 - a
        elif stage == 1:
            src = t.at[(y + d + 4) % 4] if a == 0 else t.at[:, (x + d + 4) % 4]
            dst, axis = r1, 1 - a
        elif stage == 2:
            src = (t.at[y, (x + 2) % 4] if a == 0 else t.at[(y + 2) % 4, x]).at[half(d, NB)]
            dst, axis = r2, a
        else:
            src = t.at[y, (x + d + 4) % 4] if a == 0 else t.at[(y + d + 4) % 4, x]
            dst, axis = r3, a
        return remote(
            src,
            dst.at[a, c, k],
            rs_send_sem.at[a, c, stage, k],
            rs_recv_sem.at[a, c, stage, k],
            beside(axis, d),
        )

    def add(p, q):
        return p.astype(F32) + q.astype(F32)

    def rs_start(c):
        each(lambda a, k: rs_copy(a, c, 0, k).start())

    def rs_one(c):
        def go(a, k):
            d = SIGNS[k]
            rs_copy(a, c, 0, k).wait_recv()
            if a == 0:
                yy = (y + d + 4) % 4
                t_in[c, yy, half(d, 4)] = add(t_in[c, yy, half(d, 4)], r0[a, c, k]).astype(BF16)
            else:
                xx = (x + d + 4) % 4
                t_out[c, half(d, 4), xx] = add(t_out[c, half(d, 4), xx], r0[a, c, k]).astype(BF16)
            rs_copy(a, c, 1, k).start()

        each(go)

    def rs_two(c):
        for a in range(2):
            for k in range(2):
                rs_copy(a, c, 1, k).wait_recv()
            got = add(r1[a, c, 0], r1[a, c, 1])
            if a == 0:
                t_in[c, y] = (t_in[c, y].astype(F32) + got).astype(BF16)
            else:
                t_out[c, :, x] = (t_out[c, :, x].astype(F32) + got).astype(BF16)
            for k in range(2):
                rs_copy(a, c, 2, k).start()

    def rs_three(c):
        def go(a, k):
            d = SIGNS[k]
            rs_copy(a, c, 2, k).wait_recv()
            if a == 0:
                xx = (x + d + 4) % 4
                t_in[c, y, xx, half(d, NB)] = add(t_in[c, y, xx, half(d, NB)], r2[a, c, k]).astype(BF16)
            else:
                yy = (y + d + 4) % 4
                t_out[c, yy, x, half(d, NB)] = add(t_out[c, yy, x, half(d, NB)], r2[a, c, k]).astype(BF16)
            rs_copy(a, c, 3, k).start()

        each(go)

    def z_copy(a, c):
        return remote(
            z_send.at[a, c], z_recv.at[a, c], z_send_sem.at[a, c], z_recv_sem.at[a, c], across
        )

    def rs_four(c):
        for a in range(2):
            for k in range(2):
                rs_copy(a, c, 3, k).wait_recv()
            total = add(r3[a, c, 0], r3[a, c, 1]) + (t_in, t_out)[a][c, y, x].astype(F32)
            low, high = total[:, :8], total[:, 8:]
            mine = jnp.where(zh == 0, low, high)
            other = jnp.where(zh == 0, high, low)
            z_send[a, c] = other.reshape(NB * 8, BLK).astype(BF16)
            (w_in_grad, w_out_grad)[a][c] = mine
            z_copy(a, c).start()

    def rs_last(c):
        for a in range(2):
            z_copy(a, c).wait_recv()
            out = (w_in_grad, w_out_grad)[a]
            out[c] = out[c] + z_recv[a, c].astype(F32).reshape(NB, 8, BLK)

    def place(section, g):
        near = jnp.where(section == 0, g + 1 - 2 * (g % 2), (g + 2) % 4)
        far = jnp.where(section == 2, C + g, 2 * C + g)
        return jnp.where(section < 2, near, far)

    def block(ref, g, b):
        return ref[g, :, :, b].reshape(BLK, BLK)

    def part_one(g, j):
        h = J * g + j
        ids = [g, place(kept[h, 0], g), place(kept[h, 1], g)]
        ws = [block(g_in, g, 3 * j + s) for s in range(3)]
        pre = nn(xs[ids[0]], ws[0]) + nn(xs[ids[1]], ws[1]) + nn(xs[ids[2]], ws[2])
        cdf = 0.5 * (1.0 + lax.erf(pre * 0.7071067811865476))
        act = (pre * cdf).astype(BF16)
        slope = cdf + pre * jnp.exp(-0.5 * pre * pre) * 0.3989422804014327
        vs = [block(g_out, g, 3 * j + s) for s in range(3)]
        act_grad = nt(cs[ids[0]], vs[0]) + nt(cs[ids[1]], vs[1]) + nt(cs[ids[2]], vs[2])
        pg = (act_grad * slope).astype(BF16)
        act_all[j] = act
        pg_all[j] = pg
        act_t = act.T
        for s in range(3):
            out_term = (nn(act_t, cs[ids[s]]) * scale).astype(BF16)
            t_out[g, :, :, 3 * j + s] = out_term.reshape(4, 4, 16, BLK)
            in_term = (nn(xt[ids[s]], pg) * scale).astype(BF16)
            t_in[g, :, :, 3 * j + s] = in_term.reshape(4, 4, 16, BLK)

    def far_copy(kind, p, g):
        return remote(
            far_send.at[kind, p, g],
            far_recv.at[kind, p, g],
            far_send_sem.at[kind, p, g],
            far_recv_sem.at[kind, p, g],
            peers[p],
        )

    def part_two(g):
        def pick(ref, section):
            def one(j):
                h = J * g + j
                parts = []
                for s in range(2):
                    flag = jnp.where(kept[h, s] == section, 1.0, 0.0).astype(F32)
                    parts.append(block(ref, g, 3 * j + 1 + s).astype(F32) * flag)
                return (parts[0] + parts[1]).astype(BF16)

            return [one(j) for j in range(J)]

        def own(ref):
            return [block(ref, g, 3 * j) for j in range(J)]

        def total(kind, ws):
            if kind == 0:
                act = jnp.concatenate([act_all[j] for j in range(J)], axis=1)
                return nn(act, jnp.concatenate(ws, axis=0))
            pg = jnp.concatenate([pg_all[j] for j in range(J)], axis=1)
            return nt(pg, jnp.concatenate(ws, axis=1))

        for kind in range(2):
            ref = (g_out, g_in)[kind]
            acc = (acc_m, acc_n)[kind]
            for p in range(2):
                far_send[kind, p, g] = total(kind, pick(ref, 2 + p)).astype(BF16)
                far_copy(kind, p, g).start()
            acc[g] = acc[g] + total(kind, own(ref))
            near = (g + 1 - 2 * (g % 2), (g + 2) % 4)
            for p in range(2):
                acc[near[p]] = acc[near[p]] + total(kind, pick(ref, p))

    def wait_gather(c):
        each(lambda a, k: ag_copy(a, c, 3, k).wait_recv())

    def finish():
        def out_copy(kind, g):
            stage = (act_all, pg_all)[kind]
            out = (mixed, tokens_grad)[kind]
            return pltpu.make_async_copy(
                stage.at[g], out.at[:, pl.ds(BLK * g, BLK)], local_sem.at[kind, g]
            )

        for kind in range(2):
            for g in range(C):
                for p in range(2):
                    far_copy(kind, p, g).wait_recv()
                value = (acc_m, acc_n)[kind][g] + add(far_recv[kind, 0, g], far_recv[kind, 1, g])
                (act_all, pg_all)[kind][g] = value.astype(BF16)
                out_copy(kind, g).start()
        for kind in range(2):
            for g in range(C):
                out_copy(kind, g).wait()

    def event(g, behind, fn):
        @pl.when((g >= behind) & (g < C + behind))
        def _():
            fn(g - behind)

    def compute(g):
        wait_gather(g)

        @pl.loop(0, J)
        def _(j):
            part_one(g, j)

        part_two(g)

    @pl.loop(0, C + 5)
    def _(g):
        event(g, 0, compute)

        @pl.when(g == 0)
        def _():
            ag_three(C - 1)

        event(g, 0, rs_start)
        event(g, 1, rs_one)
        event(g, 3, rs_three)
        event(g, 4, rs_four)

        @pl.when(g == C + 1)
        def _():
            finish()

        event(g, 2, rs_two)
        event(g, 5, rs_last)

    @pl.loop(0, C)
    def _(c):
        for stage in range(4):
            each(lambda a, k: ag_copy(a, c, stage, k).wait_send())
            each(lambda a, k: rs_copy(a, c, stage, k).wait_send())
        for a in range(2):
            zh_copy(a, c).wait_send()
            z_copy(a, c).wait_send()
            for p in range(2):
                tok_copy(a, p, c).wait_send()
                far_copy(a, p, c).wait_send()


def hand_over(*refs):
    n = 4
    ins, outs, bufs, (sem_in, sem_out) = refs[:n], refs[n : 2 * n], refs[2 * n : 3 * n], refs[3 * n :]
    copies = []
    for i in range(n):
        parts = 4 if i < 2 else 1
        rows = ins[i].shape[0] // parts
        for k in range(parts):
            at = pl.ds(k * rows, rows)
            copies.append(
                (
                    pltpu.make_async_copy(ins[i].at[at], bufs[i].at[at], sem_in.at[i, k]),
                    pltpu.make_async_copy(bufs[i].at[at], outs[i].at[at], sem_out.at[i, k]),
                )
            )
    for first, _ in copies:
        first.start()
    for first, second in copies:
        first.wait()
        second.start()
    for _, second in copies:
        second.wait()


def per_device(tokens, out_cot, kept, w_in, w_out):
    vmem = pl.BlockSpec(memory_space=pltpu.VMEM)
    hbm = pl.BlockSpec(memory_space=pl.ANY)
    dma = pltpu.SemaphoreType.DMA
    full = pltpu.VMEM((C, 4, 4, NB, 16, BLK), BF16)
    row = (TOK, BLK)
    results = pl.pallas_call(
        kernel,
        out_shape=(
            jax.ShapeDtypeStruct(tokens.shape, BF16),
            jax.ShapeDtypeStruct(tokens.shape, BF16),
            jax.ShapeDtypeStruct((C, NB, 8, BLK), F32),
            jax.ShapeDtypeStruct((C, NB, 8, BLK), F32),
        ),
        in_specs=[pl.BlockSpec(memory_space=pltpu.SMEM), hbm, hbm, vmem, vmem],
        out_specs=(hbm, hbm, vmem, vmem),
        scratch_shapes=[
            full,
            full,
            full,
            full,
            pltpu.VMEM((2, C, 2, 2, NB, 16, BLK), BF16),
            pltpu.VMEM((2, C, 2, 4, NB, 16, BLK), BF16),
            pltpu.VMEM((2, C, 2, NB // 2, 16, BLK), BF16),
            pltpu.VMEM((2, C, 2, NB, 16, BLK), BF16),
            pltpu.VMEM((2, C * NB * 8, BLK), BF16),
            pltpu.VMEM((2, C, NB * 8, BLK), BF16),
            pltpu.VMEM((2, C, NB * 8, BLK), BF16),
            pltpu.VMEM((3 * C,) + row, BF16),
            pltpu.VMEM((3 * C,) + row, BF16),
            pltpu.VMEM((3 * C, BLK, TOK), BF16),
            pltpu.VMEM((C,) + row, F32),
            pltpu.VMEM((C,) + row, F32),
            pltpu.VMEM((2, 2, C) + row, BF16),
            pltpu.VMEM((2, 2, C) + row, BF16),
            pltpu.VMEM((J,) + row, BF16),
            pltpu.VMEM((J,) + row, BF16),
            dma((2, C, 4, 2)),
            dma((2, C, 4, 2)),
            dma((2, C, 4, 2)),
            dma((2, C, 4, 2)),
            dma((2, C)),
            dma((2, C)),
            dma((2, 2, C)),
            dma((2, 2, C)),
            dma((2, 2, C)),
            dma((2, 2, C)),
            dma((2, C)),
            dma((2, C)),
            dma((2, C)),
        ],
        compiler_params=pltpu.CompilerParams(
            collective_id=0, has_side_effects=True, vmem_limit_bytes=64 * 2**20
        ),
        cost_estimate=pl.CostEstimate(
            flops=24 * 10**9, bytes_accessed=8 * 2**20, transcendentals=4 * 2**20
        ),
    )(kept, tokens, out_cot, w_in.reshape(C * NB * 8, BLK), w_out.reshape(C * NB * 8, BLK))
    mixed, tokens_grad, w_in_grad, w_out_grad = pl.pallas_call(
        hand_over,
        out_shape=tuple(jax.ShapeDtypeStruct(r.shape, r.dtype) for r in results),
        in_specs=[hbm] * 4,
        out_specs=(hbm,) * 4,
        scratch_shapes=[pltpu.VMEM(r.shape, r.dtype) for r in results] + [dma((4, 4)), dma((4, 4))],
    )(*results)
    shape = w_in.shape
    return mixed, tokens_grad, w_in_grad.reshape(shape), w_out_grad.reshape(shape)


def solution(mesh):
    wide, blocks = P("dp", "tensor"), P("tensor", None, "dp", None)
    return jax.shard_map(
        per_device,
        mesh=mesh,
        in_specs=(wide, wide, P("tensor", None), blocks, blocks),
        out_specs=(wide, wide, blocks, blocks),
        check_vma=False,
    )
```

```python
import functools

import jax
import jax.numpy as jnp
from jax import lax
from jax.experimental import pallas as pl
from jax.experimental.pallas import tpu as pltpu
from jax.sharding import PartitionSpec as P

MESH = pl.DeviceIdType.MESH
F32, BF16 = jnp.float32, jnp.bfloat16
C = 4
J = 4
NB = 12
R = 2 * C
RB = NB // 2
EARLY = 3
BLK = 256
TOK = 512
SIGNS = (1, -1)


def nn(a, b):
    return lax.dot_general(a, b, (((1,), (0,)), ((), ())), preferred_element_type=F32)


def nt(a, b):
    return lax.dot_general(a, b, (((1,), (1,)), ((), ())), preferred_element_type=F32)


def kernel(
    kept,
    tokens,
    out_cot,
    w_in,
    w_out,
    mixed,
    tokens_grad,
    w_in_grad,
    w_out_grad,
    g_in,
    g_out,
    t_in,
    t_out,
    r0,
    r1,
    r2,
    r3,
    zh_recv,
    z_send,
    z_recv,
    xs,
    cs,
    xt,
    xs_far,
    cs_far,
    xt_far,
    acc_m,
    acc_n,
    far_send,
    far_recv,
    act_all,
    pg_all,
    ag_send_sem,
    ag_recv_sem,
    rs_send_sem,
    rs_recv_sem,
    zh_send_sem,
    zh_recv_sem,
    tok_send_sem,
    tok_recv_sem,
    far_send_sem,
    far_recv_sem,
    z_send_sem,
    z_recv_sem,
    local_sem,
):
    dp = lax.axis_index("dp")
    te = lax.axis_index("tensor")
    y, x, zh = dp // 8, (dp // 2) % 4, dp % 2
    scale = float(TOK * 32) ** -0.5

    def at(yy, xx, zz):
        return {"dp": (yy % 4) * 8 + (xx % 4) * 2 + zz}

    def beside(axis, d):
        return at(y, x + d + 4, zh) if axis == 0 else at(y + d + 4, x, zh)

    across = {"dp": dp + 1 - 2 * zh}
    core_peer = {"tensor": te + 1 - 2 * (te % 2)}
    z_peer = {"tensor": (te + 2) % 4}
    peers = (core_peer, z_peer)

    def remote(src, dst, send, recv, to):
        return pltpu.make_async_remote_copy(
            src_ref=src, dst_ref=dst, send_sem=send, recv_sem=recv, device_id=to, device_id_type=MESH
        )

    def load(kind, i):
        src, dst = ((tokens, xs), (out_cot, cs))[kind]
        return pltpu.make_async_copy(
            src.at[:, pl.ds(BLK * i, BLK)], dst.at[i], local_sem.at[kind, i]
        )

    for kind in range(2):
        for i in range(C):
            load(kind, i).start()

    barrier = pltpu.get_barrier_semaphore()
    everyone = [across, core_peer, z_peer] + [beside(a, d) for a in (0, 1) for d in SIGNS]
    for to in everyone:
        pl.semaphore_signal(barrier, inc=1, device_id=to, device_id_type=MESH)
    pl.semaphore_wait(barrier, len(everyone))

    def zh_copy(a, c):
        rows = pl.ds(c * NB * 8, NB * 8)
        return remote(
            (w_in, w_out)[a].at[rows],
            zh_recv.at[a, rows],
            zh_send_sem.at[a, c],
            zh_recv_sem.at[a, c],
            across,
        )

    for c in range(C):
        for a in range(2):
            zh_copy(a, c).start()

    def tok_copy(kind, p, i):
        return remote(
            (xs, cs)[kind].at[i],
            (xs_far, cs_far)[kind].at[p, i],
            tok_send_sem.at[kind, p, i],
            tok_recv_sem.at[kind, p, i],
            peers[p],
        )

    for kind in range(2):
        for i in range(C):
            load(kind, i).wait()

    def join(a, c):
        rows = pl.ds(c * NB * 8, NB * 8)
        own = (w_in, w_out)[a][rows].astype(F32).reshape(NB, 8, BLK)
        got = zh_recv[a, rows].astype(F32).reshape(NB, 8, BLK)
        low = jnp.where(zh == 0, own, got)
        high = jnp.where(zh == 0, got, own)
        (g_in, g_out)[a][c, y, x] = jnp.concatenate([low, high], axis=1).astype(BF16)

    def opposite(v, d):
        return (v - d + 4) % 4

    def half(d, n):
        return pl.ds(0, n // 2) if d == 1 else pl.ds(n // 2, n // 2)

    def ag_copy(a, c, stage, k):
        d = SIGNS[k]
        g = (g_in, g_out)[a].at[c]
        if stage == 0:
            ref, axis = g.at[y, x], a
        elif stage == 1:
            ref = (g.at[y, opposite(x, d)] if a == 0 else g.at[opposite(y, d), x]).at[half(d, NB)]
            axis = a
        elif stage == 2:
            ref, axis = (g.at[y] if a == 0 else g.at[:, x]), 1 - a
        else:
            ref = g.at[opposite(y, d), half(d, 4)] if a == 0 else g.at[half(d, 4), opposite(x, d)]
            axis = 1 - a
        return remote(
            ref, ref, ag_send_sem.at[a, c, stage, k], ag_recv_sem.at[a, c, stage, k], beside(axis, d)
        )

    def each(fn):
        for a in range(2):
            for k in range(2):
                fn(a, k)

    def transpose(i):
        xt[i] = xs[i].T

    def ag_zero(c):
        for a in range(2):
            zh_copy(a, c).wait_recv()
            join(a, c)
            for k in range(2):
                ag_copy(a, c, 0, k).start()
        for kind in range(2):
            for p in range(2):
                tok_copy(kind, p, c).start()

    def ag_next(stage):
        def go(c):
            for a in range(2):
                for k in range(2):
                    ag_copy(a, c, stage - 1, k).wait_recv()
                    if stage != 2:
                        ag_copy(a, c, stage, k).start()
                if stage == 2:
                    for k in range(2):
                        ag_copy(a, c, stage, k).start()

        return go

    def event(t, behind, fn, count=C):
        @pl.when((t >= behind) & (t < count + behind))
        def _():
            fn(t - behind)

    @pl.loop(0, C + 2)
    def _(t):
        event(t, 0, ag_zero)
        event(t, 1, ag_next(1))
        event(t, 2, ag_next(2))
        event(t, 3, ag_next(3), EARLY)
        event(t, 0, transpose)

    acc_m[...] = jnp.zeros_like(acc_m)
    acc_n[...] = jnp.zeros_like(acc_n)

    def rs_copy(a, c, stage, k):
        d = SIGNS[k]
        t = (t_in, t_out)[a].at[c]
        if stage == 0:
            src = t.at[(y + 2) % 4, half(d, 4)] if a == 0 else t.at[half(d, 4), (x + 2) % 4]
            dst, axis = r0, 1 - a
        elif stage == 1:
            src = t.at[(y + d + 4) % 4] if a == 0 else t.at[:, (x + d + 4) % 4]
            dst, axis = r1, 1 - a
        elif stage == 2:
            src = (t.at[y, (x + 2) % 4] if a == 0 else t.at[(y + 2) % 4, x]).at[half(d, RB)]
            dst, axis = r2, a
        else:
            src = t.at[y, (x + d + 4) % 4] if a == 0 else t.at[(y + d + 4) % 4, x]
            dst, axis = r3, a
        return remote(
            src,
            dst.at[a, c, k],
            rs_send_sem.at[a, c, stage, k],
            rs_recv_sem.at[a, c, stage, k],
            beside(axis, d),
        )

    def add(p, q):
        return p.astype(F32) + q.astype(F32)

    def rs_start(c):
        each(lambda a, k: rs_copy(a, c, 0, k).start())

    def rs_one(c):
        def go(a, k):
            d = SIGNS[k]
            rs_copy(a, c, 0, k).wait_recv()
            if a == 0:
                yy = (y + d + 4) % 4
                t_in[c, yy, half(d, 4)] = add(t_in[c, yy, half(d, 4)], r0[a, c, k]).astype(BF16)
            else:
                xx = (x + d + 4) % 4
                t_out[c, half(d, 4), xx] = add(t_out[c, half(d, 4), xx], r0[a, c, k]).astype(BF16)
            rs_copy(a, c, 1, k).start()

        each(go)

    def rs_two(c):
        for a in range(2):
            for k in range(2):
                rs_copy(a, c, 1, k).wait_recv()
            got = add(r1[a, c, 0], r1[a, c, 1])
            if a == 0:
                t_in[c, y] = (t_in[c, y].astype(F32) + got).astype(BF16)
            else:
                t_out[c, :, x] = (t_out[c, :, x].astype(F32) + got).astype(BF16)
            for k in range(2):
                rs_copy(a, c, 2, k).start()

    def rs_three(c):
        def go(a, k):
            d = SIGNS[k]
            rs_copy(a, c, 2, k).wait_recv()
            if a == 0:
                xx = (x + d + 4) % 4
                t_in[c, y, xx, half(d, RB)] = add(t_in[c, y, xx, half(d, RB)], r2[a, c, k]).astype(BF16)
            else:
                yy = (y + d + 4) % 4
                t_out[c, yy, x, half(d, RB)] = add(t_out[c, yy, x, half(d, RB)], r2[a, c, k]).astype(BF16)
            rs_copy(a, c, 3, k).start()

        each(go)

    def z_copy(a, c):
        return remote(
            z_send.at[a, c], z_recv.at[a, c], z_send_sem.at[a, c], z_recv_sem.at[a, c], across
        )

    def rs_four(c):
        for a in range(2):
            for k in range(2):
                rs_copy(a, c, 3, k).wait_recv()
            total = add(r3[a, c, 0], r3[a, c, 1]) + (t_in, t_out)[a][c, y, x].astype(F32)
            low, high = total[:, :8], total[:, 8:]
            mine = jnp.where(zh == 0, low, high)
            other = jnp.where(zh == 0, high, low)
            z_send[a, c] = other.reshape(RB * 8, BLK).astype(BF16)
            (w_in_grad, w_out_grad)[a][c] = mine
            z_copy(a, c).start()

    def rs_last(c):
        for a in range(2):
            z_copy(a, c).wait_recv()
            out = (w_in_grad, w_out_grad)[a]
            out[c] = out[c] + z_recv[a, c].astype(F32).reshape(RB, 8, BLK)

    def choose(near, far, section, g):
        other = jnp.where(section == 0, g + 1 - 2 * (g % 2), (g + 2) % 4)
        return jnp.where(
            section < 2, near[other], jnp.where(section == 2, far[0, g], far[1, g])
        )

    def block(ref, g, b):
        return ref[g, :, :, b].reshape(BLK, BLK)

    def part_one(g, j):
        h = J * g + j
        x_s, c_s, t_s = [
            [near[g]] + [choose(near, far, kept[s, h], g) for s in range(2)]
            for near, far in ((xs, xs_far), (cs, cs_far), (xt, xt_far))
        ]
        ws = [block(g_in, g, 3 * j + s) for s in range(3)]
        pre = nn(x_s[0], ws[0]) + nn(x_s[1], ws[1]) + nn(x_s[2], ws[2])
        cdf = 0.5 * (1.0 + lax.erf(pre * 0.7071067811865476))
        act = (pre * cdf).astype(BF16)
        slope = cdf + pre * jnp.exp(-0.5 * pre * pre) * 0.3989422804014327
        vs = [block(g_out, g, 3 * j + s) for s in range(3)]
        act_grad = nt(c_s[0], vs[0]) + nt(c_s[1], vs[1]) + nt(c_s[2], vs[2])
        pg = (act_grad * slope).astype(BF16)
        act_all[j] = act
        pg_all[j] = pg
        act_t = act.T
        for s in range(3):
            out_term = (nn(act_t, c_s[s]) * scale).astype(BF16)
            t_out[2 * g + j // 2, :, :, 3 * (j % 2) + s] = out_term.reshape(4, 4, 16, BLK)
            in_term = (nn(t_s[s], pg) * scale).astype(BF16)
            t_in[2 * g + j // 2, :, :, 3 * (j % 2) + s] = in_term.reshape(4, 4, 16, BLK)

    def far_copy(kind, p, g):
        return remote(
            far_send.at[kind, p, g],
            far_recv.at[kind, p, g],
            far_send_sem.at[kind, p, g],
            far_recv_sem.at[kind, p, g],
            peers[p],
        )

    def part_two(g):
        def pick(ref, section):
            def one(j):
                h = J * g + j
                parts = []
                for s in range(2):
                    flag = jnp.where(kept[s, h] == section, 1.0, 0.0).astype(F32)
                    parts.append(block(ref, g, 3 * j + 1 + s).astype(F32) * flag)
                return (parts[0] + parts[1]).astype(BF16)

            return [one(j) for j in range(J)]

        def own(ref):
            return [block(ref, g, 3 * j) for j in range(J)]

        def total(kind, ws):
            if kind == 0:
                act = jnp.concatenate([act_all[j] for j in range(J)], axis=1)
                return nn(act, jnp.concatenate(ws, axis=0))
            pg = jnp.concatenate([pg_all[j] for j in range(J)], axis=1)
            return nt(pg, jnp.concatenate(ws, axis=1))

        for kind in range(2):
            ref = (g_out, g_in)[kind]
            acc = (acc_m, acc_n)[kind]
            for p in range(2):
                far_send[kind, p, g] = total(kind, pick(ref, 2 + p)).astype(BF16)
                far_copy(kind, p, g).start()
            acc[g] = acc[g] + total(kind, own(ref))
            near = (g + 1 - 2 * (g % 2), (g + 2) % 4)
            for p in range(2):
                acc[near[p]] = acc[near[p]] + total(kind, pick(ref, p))

    def wait_gather(c):
        each(lambda a, k: ag_copy(a, c, 3, k).wait_recv())

    def finish():
        def out_copy(kind, g):
            stage = (act_all, pg_all)[kind]
            out = (mixed, tokens_grad)[kind]
            return pltpu.make_async_copy(
                stage.at[g], out.at[:, pl.ds(BLK * g, BLK)], local_sem.at[kind, g]
            )

        for kind in range(2):
            for g in range(C):
                for p in range(2):
                    far_copy(kind, p, g).wait_recv()
                    far_copy(kind, p, g).wait_send()
                value = (acc_m, acc_n)[kind][g] + add(far_recv[kind, 0, g], far_recv[kind, 1, g])
                (act_all, pg_all)[kind][g] = value.astype(BF16)
                out_copy(kind, g).start()
        for kind in range(2):
            for g in range(C):
                out_copy(kind, g).wait()

    def compute(u):
        g = u // 2

        @pl.when(u % 2 == 0)
        def _():
            for kind in range(2):
                for p in range(2):
                    tok_copy(kind, p, g).wait_recv()
            for p in range(2):
                xt_far[p, g] = xs_far[p, g].T
            wait_gather(g)

        @pl.loop(2 * (u % 2), 2 * (u % 2) + 2)
        def _(j):
            part_one(g, j)

    def compute_two(u):
        @pl.when(u % 2 == 1)
        def _():
            part_two(u // 2)

    def gather_sent(c):
        for stage in range(4):
            each(lambda a, k: ag_copy(a, c, stage, k).wait_send())
        for a in range(2):
            zh_copy(a, c).wait_send()
            for p in range(2):
                tok_copy(a, p, c).wait_send()

    def scatter_sent(c):
        for stage in range(4):
            each(lambda a, k: rs_copy(a, c, stage, k).wait_send())
        for a in range(2):
            z_copy(a, c).wait_send()

    @pl.loop(0, R + 6)
    def _(u):
        event(u, 0, compute, R)

        @pl.when((u % 2 == 1) & (u < 2 * (C - EARLY)))
        def _():
            ag_next(3)(EARLY + u // 2)

        event(u, 0, rs_start, R)
        event(u, 2, rs_one, R)
        event(u, 0, compute_two, R)
        event(u, 4, rs_three, R)
        event(u, 5, rs_four, R)

        @pl.when(u == R + 2)
        def _():
            finish()

        event(u, 3, rs_two, R)
        event(u, 6, rs_last, R)
        event(u, 6, scatter_sent, R)
        event(u, 4, gather_sent)


def hand_over(*refs):
    n = 4
    ins, outs, bufs, (sem_in, sem_out) = refs[:n], refs[n : 2 * n], refs[2 * n : 3 * n], refs[3 * n :]
    copies = []
    for i in range(n):
        parts = 4 if i < 2 else 1
        rows = ins[i].shape[0] // parts
        for k in range(parts):
            at = pl.ds(k * rows, rows)
            copies.append(
                (
                    pltpu.make_async_copy(ins[i].at[at], bufs[i].at[at], sem_in.at[i, k]),
                    pltpu.make_async_copy(bufs[i].at[at], outs[i].at[at], sem_out.at[i, k]),
                )
            )
    for first, _ in copies:
        first.start()
    for first, second in copies:
        first.wait()
        second.start()
    for _, second in copies:
        second.wait()


def per_device(tokens, out_cot, kept, w_in, w_out):
    vmem = pl.BlockSpec(memory_space=pltpu.VMEM)
    hbm = pl.BlockSpec(memory_space=pl.ANY)
    dma = pltpu.SemaphoreType.DMA
    full = pltpu.VMEM((C, 4, 4, NB, 16, BLK), BF16)
    term = pltpu.VMEM((R, 4, 4, RB, 16, BLK), BF16)
    row = (TOK, BLK)
    results = pl.pallas_call(
        kernel,
        out_shape=(
            jax.ShapeDtypeStruct(tokens.shape, BF16),
            jax.ShapeDtypeStruct(tokens.shape, BF16),
            jax.ShapeDtypeStruct((R, RB, 8, BLK), F32),
            jax.ShapeDtypeStruct((R, RB, 8, BLK), F32),
        ),
        in_specs=[pl.BlockSpec(memory_space=pltpu.SMEM), hbm, hbm, vmem, vmem],
        out_specs=(hbm, hbm, vmem, vmem),
        scratch_shapes=[
            full,
            full,
            term,
            term,
            pltpu.VMEM((2, R, 2, 2, RB, 16, BLK), BF16),
            pltpu.VMEM((2, R, 2, 4, RB, 16, BLK), BF16),
            pltpu.VMEM((2, R, 2, RB // 2, 16, BLK), BF16),
            pltpu.VMEM((2, R, 2, RB, 16, BLK), BF16),
            pltpu.VMEM((2, C * NB * 8, BLK), BF16),
            pltpu.VMEM((2, R, RB * 8, BLK), BF16),
            pltpu.VMEM((2, R, RB * 8, BLK), BF16),
            pltpu.VMEM((C,) + row, BF16),
            pltpu.VMEM((C,) + row, BF16),
            pltpu.VMEM((C, BLK, TOK), BF16),
            pltpu.VMEM((2, C) + row, BF16),
            pltpu.VMEM((2, C) + row, BF16),
            pltpu.VMEM((2, C, BLK, TOK), BF16),
            pltpu.VMEM((C,) + row, F32),
            pltpu.VMEM((C,) + row, F32),
            pltpu.VMEM((2, 2, C) + row, BF16),
            pltpu.VMEM((2, 2, C) + row, BF16),
            pltpu.VMEM((J,) + row, BF16),
            pltpu.VMEM((J,) + row, BF16),
            dma((2, C, 4, 2)),
            dma((2, C, 4, 2)),
            dma((2, R, 4, 2)),
            dma((2, R, 4, 2)),
            dma((2, C)),
            dma((2, C)),
            dma((2, 2, C)),
            dma((2, 2, C)),
            dma((2, 2, C)),
            dma((2, 2, C)),
            dma((2, R)),
            dma((2, R)),
            dma((2, C)),
        ],
        compiler_params=pltpu.CompilerParams(
            collective_id=0, has_side_effects=True, vmem_limit_bytes=64 * 2**20
        ),
        cost_estimate=pl.CostEstimate(
            flops=24 * 10**9, bytes_accessed=8 * 2**20, transcendentals=4 * 2**20
        ),
    )(kept.T, tokens, out_cot, w_in.reshape(C * NB * 8, BLK), w_out.reshape(C * NB * 8, BLK))
    mixed, tokens_grad, w_in_grad, w_out_grad = pl.pallas_call(
        hand_over,
        out_shape=tuple(jax.ShapeDtypeStruct(r.shape, r.dtype) for r in results),
        in_specs=[hbm] * 4,
        out_specs=(hbm,) * 4,
        scratch_shapes=[pltpu.VMEM(r.shape, r.dtype) for r in results] + [dma((4, 4)), dma((4, 4))],
    )(*results)
    shape = w_in.shape
    return mixed, tokens_grad, w_in_grad.reshape(shape), w_out_grad.reshape(shape)


def solution(mesh):
    wide, blocks = P("dp", "tensor"), P("tensor", None, "dp", None)
    return jax.shard_map(
        per_device,
        mesh=mesh,
        in_specs=(wide, wide, P("tensor", None), blocks, blocks),
        out_specs=(wide, wide, blocks, blocks),
        check_vma=False,
    )
```

```python
import functools

import jax
import jax.numpy as jnp
from jax import lax
from jax.experimental import pallas as pl
from jax.experimental.pallas import tpu as pltpu
from jax.sharding import PartitionSpec as P

MESH = pl.DeviceIdType.MESH
F32, BF16 = jnp.float32, jnp.bfloat16
C = 4
J = 4
NB = 12
R = 2 * C
RB = NB // 2
EARLY = 3
BLK = 256
TOK = 512
SIGNS = (1, -1)


def nn(a, b):
    return lax.dot_general(a, b, (((1,), (0,)), ((), ())), preferred_element_type=F32)


def nt(a, b):
    return lax.dot_general(a, b, (((1,), (1,)), ((), ())), preferred_element_type=F32)


def kernel(
    kept,
    tokens,
    out_cot,
    w_in,
    w_out,
    mixed,
    tokens_grad,
    w_in_grad,
    w_out_grad,
    g_in,
    g_out,
    t_in,
    t_out,
    r0,
    r1,
    r2,
    r3,
    zh_recv,
    z_send,
    z_recv,
    xs,
    cs,
    xt,
    xs_far,
    cs_far,
    xt_far,
    acc_m,
    acc_n,
    far_send,
    far_recv,
    act_all,
    pg_all,
    ag_send_sem,
    ag_recv_sem,
    rs_send_sem,
    rs_recv_sem,
    zh_send_sem,
    zh_recv_sem,
    tok_send_sem,
    tok_recv_sem,
    far_send_sem,
    far_recv_sem,
    z_send_sem,
    z_recv_sem,
    local_sem,
):
    dp = lax.axis_index("dp")
    te = lax.axis_index("tensor")
    y, x, zh = dp // 8, (dp // 2) % 4, dp % 2
    scale = float(TOK * 32) ** -0.5

    def at(yy, xx, zz):
        return {"dp": (yy % 4) * 8 + (xx % 4) * 2 + zz}

    def beside(axis, d):
        return at(y, x + d + 4, zh) if axis == 0 else at(y + d + 4, x, zh)

    across = {"dp": dp + 1 - 2 * zh}
    core_peer = {"tensor": te + 1 - 2 * (te % 2)}
    z_peer = {"tensor": (te + 2) % 4}
    peers = (core_peer, z_peer)

    def remote(src, dst, send, recv, to):
        return pltpu.make_async_remote_copy(
            src_ref=src, dst_ref=dst, send_sem=send, recv_sem=recv, device_id=to, device_id_type=MESH
        )

    def load(kind, i):
        src, dst = ((tokens, xs), (out_cot, cs))[kind]
        return pltpu.make_async_copy(
            src.at[:, pl.ds(BLK * i, BLK)], dst.at[i], local_sem.at[kind, i]
        )

    for kind in range(2):
        for i in range(C):
            load(kind, i).start()

    barrier = pltpu.get_barrier_semaphore()
    everyone = [across, core_peer, z_peer] + [beside(a, d) for a in (0, 1) for d in SIGNS]
    for to in everyone:
        pl.semaphore_signal(barrier, inc=1, device_id=to, device_id_type=MESH)
    pl.semaphore_wait(barrier, len(everyone))

    def zh_copy(a, c):
        rows = pl.ds(c * NB * 8, NB * 8)
        return remote(
            (w_in, w_out)[a].at[rows],
            zh_recv.at[a, rows],
            zh_send_sem.at[a, c],
            zh_recv_sem.at[a, c],
            across,
        )

    for c in range(C):
        for a in range(2):
            zh_copy(a, c).start()

    def tok_copy(kind, p, i):
        return remote(
            (xs, cs)[kind].at[i],
            (xs_far, cs_far)[kind].at[p, i],
            tok_send_sem.at[kind, p, i],
            tok_recv_sem.at[kind, p, i],
            peers[p],
        )

    for kind in range(2):
        for i in range(C):
            load(kind, i).wait()

    def join(a, c):
        rows = pl.ds(c * NB * 8, NB * 8)
        own = (w_in, w_out)[a][rows].astype(F32).reshape(NB, 8, BLK)
        got = zh_recv[a, rows].astype(F32).reshape(NB, 8, BLK)
        low = jnp.where(zh == 0, own, got)
        high = jnp.where(zh == 0, got, own)
        (g_in, g_out)[a][c, y, x] = jnp.concatenate([low, high], axis=1).astype(BF16)

    def opposite(v, d):
        return (v - d + 4) % 4

    def half(d, n):
        return pl.ds(0, n // 2) if d == 1 else pl.ds(n // 2, n // 2)

    def ag_copy(a, c, stage, k):
        d = SIGNS[k]
        g = (g_in, g_out)[a].at[c]
        if stage == 0:
            ref, axis = g.at[y, x], a
        elif stage == 1:
            ref = (g.at[y, opposite(x, d)] if a == 0 else g.at[opposite(y, d), x]).at[half(d, NB)]
            axis = a
        elif stage == 2:
            ref, axis = (g.at[y] if a == 0 else g.at[:, x]), 1 - a
        else:
            ref = g.at[opposite(y, d), half(d, 4)] if a == 0 else g.at[half(d, 4), opposite(x, d)]
            axis = 1 - a
        return remote(
            ref, ref, ag_send_sem.at[a, c, stage, k], ag_recv_sem.at[a, c, stage, k], beside(axis, d)
        )

    def each(fn):
        for a in range(2):
            for k in range(2):
                fn(a, k)

    def transpose(i):
        xt[i] = xs[i].T

    def ag_zero(c):
        for a in range(2):
            zh_copy(a, c).wait_recv()
            join(a, c)
            for k in range(2):
                ag_copy(a, c, 0, k).start()
        for kind in range(2):
            for p in range(2):
                tok_copy(kind, p, c).start()

    def ag_next(stage):
        def go(c):
            for a in range(2):
                for k in range(2):
                    ag_copy(a, c, stage - 1, k).wait_recv()
                    if stage != 2:
                        ag_copy(a, c, stage, k).start()
                if stage == 2:
                    for k in range(2):
                        ag_copy(a, c, stage, k).start()

        return go

    def event(t, behind, fn, count=C):
        @pl.when((t >= behind) & (t < count + behind))
        def _():
            fn(t - behind)

    @pl.loop(0, C + 2)
    def _(t):
        event(t, 0, ag_zero)
        event(t, 1, ag_next(1))
        event(t, 2, ag_next(2))
        event(t, 3, ag_next(3), EARLY)
        event(t, 0, transpose)

    acc_m[...] = jnp.zeros_like(acc_m)
    acc_n[...] = jnp.zeros_like(acc_n)

    def rs_copy(a, c, stage, k):
        d = SIGNS[k]
        t = (t_in, t_out)[a].at[c]
        if stage == 0:
            src = t.at[(y + 2) % 4, half(d, 4)] if a == 0 else t.at[half(d, 4), (x + 2) % 4]
            dst, axis = r0, 1 - a
        elif stage == 1:
            src = t.at[(y + d + 4) % 4] if a == 0 else t.at[:, (x + d + 4) % 4]
            dst, axis = r1, 1 - a
        elif stage == 2:
            src = (t.at[y, (x + 2) % 4] if a == 0 else t.at[(y + 2) % 4, x]).at[half(d, RB)]
            dst, axis = r2, a
        else:
            src = t.at[y, (x + d + 4) % 4] if a == 0 else t.at[(y + d + 4) % 4, x]
            dst, axis = r3, a
        return remote(
            src,
            dst.at[a, c, k],
            rs_send_sem.at[a, c, stage, k],
            rs_recv_sem.at[a, c, stage, k],
            beside(axis, d),
        )

    def add(p, q):
        return p.astype(F32) + q.astype(F32)

    def rs_start(c):
        each(lambda a, k: rs_copy(a, c, 0, k).start())

    def rs_one(c):
        def go(a, k):
            d = SIGNS[k]
            rs_copy(a, c, 0, k).wait_recv()
            if a == 0:
                yy = (y + d + 4) % 4
                t_in[c, yy, half(d, 4)] = add(t_in[c, yy, half(d, 4)], r0[a, c, k]).astype(BF16)
            else:
                xx = (x + d + 4) % 4
                t_out[c, half(d, 4), xx] = add(t_out[c, half(d, 4), xx], r0[a, c, k]).astype(BF16)
            rs_copy(a, c, 1, k).start()

        each(go)

    def rs_two(c):
        for a in range(2):
            for k in range(2):
                rs_copy(a, c, 1, k).wait_recv()
            got = add(r1[a, c, 0], r1[a, c, 1])
            if a == 0:
                t_in[c, y] = (t_in[c, y].astype(F32) + got).astype(BF16)
            else:
                t_out[c, :, x] = (t_out[c, :, x].astype(F32) + got).astype(BF16)
            for k in range(2):
                rs_copy(a, c, 2, k).start()

    def rs_three(c):
        def go(a, k):
            d = SIGNS[k]
            rs_copy(a, c, 2, k).wait_recv()
            if a == 0:
                xx = (x + d + 4) % 4
                t_in[c, y, xx, half(d, RB)] = add(t_in[c, y, xx, half(d, RB)], r2[a, c, k]).astype(BF16)
            else:
                yy = (y + d + 4) % 4
                t_out[c, yy, x, half(d, RB)] = add(t_out[c, yy, x, half(d, RB)], r2[a, c, k]).astype(BF16)
            rs_copy(a, c, 3, k).start()

        each(go)

    def z_copy(a, c):
        return remote(
            z_send.at[a, c], z_recv.at[a, c], z_send_sem.at[a, c], z_recv_sem.at[a, c], across
        )

    def rs_four(c):
        for a in range(2):
            for k in range(2):
                rs_copy(a, c, 3, k).wait_recv()
            total = add(r3[a, c, 0], r3[a, c, 1]) + (t_in, t_out)[a][c, y, x].astype(F32)
            low, high = total[:, :8], total[:, 8:]
            mine = jnp.where(zh == 0, low, high)
            other = jnp.where(zh == 0, high, low)
            z_send[a, c] = other.reshape(RB * 8, BLK).astype(BF16)
            (w_in_grad, w_out_grad)[a][c] = mine
            z_copy(a, c).start()

    def rs_last(c):
        for a in range(2):
            z_copy(a, c).wait_recv()
            out = (w_in_grad, w_out_grad)[a]
            out[c] = out[c] + z_recv[a, c].astype(F32).reshape(RB, 8, BLK)

    def choose(near, far, section, g):
        other = jnp.where(section == 0, g + 1 - 2 * (g % 2), (g + 2) % 4)
        return jnp.where(
            section < 2, near[other], jnp.where(section == 2, far[0, g], far[1, g])
        )

    def block(ref, g, b):
        return ref[g, :, :, b].reshape(BLK, BLK)

    def part_one(g, j):
        h = J * g + j
        x_s, c_s, t_s = [
            [near[g]] + [choose(near, far, kept[s, h], g) for s in range(2)]
            for near, far in ((xs, xs_far), (cs, cs_far), (xt, xt_far))
        ]
        ws = [block(g_in, g, 3 * j + s) for s in range(3)]
        pre = nn(x_s[0], ws[0]) + nn(x_s[1], ws[1]) + nn(x_s[2], ws[2])
        cdf = 0.5 * (1.0 + lax.erf(pre * 0.7071067811865476))
        act = (pre * cdf).astype(BF16)
        slope = cdf + pre * jnp.exp(-0.5 * pre * pre) * 0.3989422804014327
        vs = [block(g_out, g, 3 * j + s) for s in range(3)]
        act_grad = nt(c_s[0], vs[0]) + nt(c_s[1], vs[1]) + nt(c_s[2], vs[2])
        pg = (act_grad * slope).astype(BF16)
        act_all[j] = act
        pg_all[j] = pg
        act_t = act.T
        for s in range(3):
            out_term = (nn(act_t, c_s[s]) * scale).astype(BF16)
            t_out[2 * g + j // 2, :, :, 3 * (j % 2) + s] = out_term.reshape(4, 4, 16, BLK)
            in_term = (nn(t_s[s], pg) * scale).astype(BF16)
            t_in[2 * g + j // 2, :, :, 3 * (j % 2) + s] = in_term.reshape(4, 4, 16, BLK)

    def far_copy(kind, p, g):
        return remote(
            far_send.at[kind, p, g],
            far_recv.at[kind, p, g],
            far_send_sem.at[kind, p, g],
            far_recv_sem.at[kind, p, g],
            peers[p],
        )

    def part_two(g):
        def pick(ref, section):
            def one(j):
                h = J * g + j
                parts = []
                for s in range(2):
                    flag = jnp.where(kept[s, h] == section, 1.0, 0.0).astype(F32)
                    parts.append(block(ref, g, 3 * j + 1 + s).astype(F32) * flag)
                return (parts[0] + parts[1]).astype(BF16)

            return [one(j) for j in range(J)]

        def own(ref):
            return [block(ref, g, 3 * j) for j in range(J)]

        def total(kind, ws):
            if kind == 0:
                act = jnp.concatenate([act_all[j] for j in range(J)], axis=1)
                return nn(act, jnp.concatenate(ws, axis=0))
            pg = jnp.concatenate([pg_all[j] for j in range(J)], axis=1)
            return nt(pg, jnp.concatenate(ws, axis=1))

        for kind in range(2):
            ref = (g_out, g_in)[kind]
            acc = (acc_m, acc_n)[kind]
            for p in range(2):
                far_send[kind, p, g] = total(kind, pick(ref, 2 + p)).astype(BF16)
                far_copy(kind, p, g).start()
            acc[g] = acc[g] + total(kind, own(ref))
            near = (g + 1 - 2 * (g % 2), (g + 2) % 4)
            for p in range(2):
                acc[near[p]] = acc[near[p]] + total(kind, pick(ref, p))

    def wait_gather(c):
        each(lambda a, k: ag_copy(a, c, 3, k).wait_recv())

    def finish():
        def out_copy(kind, g):
            stage = (act_all, pg_all)[kind]
            out = (mixed, tokens_grad)[kind]
            return pltpu.make_async_copy(
                stage.at[g], out.at[:, pl.ds(BLK * g, BLK)], local_sem.at[kind, g]
            )

        for kind in range(2):
            for g in range(C):
                for p in range(2):
                    far_copy(kind, p, g).wait_recv()
                    far_copy(kind, p, g).wait_send()
                value = (acc_m, acc_n)[kind][g] + add(far_recv[kind, 0, g], far_recv[kind, 1, g])
                (act_all, pg_all)[kind][g] = value.astype(BF16)
                out_copy(kind, g).start()
        for kind in range(2):
            for g in range(C):
                out_copy(kind, g).wait()

    def compute(u):
        g = u // 2

        @pl.when(u % 2 == 0)
        def _():
            for kind in range(2):
                for p in range(2):
                    tok_copy(kind, p, g).wait_recv()
            for p in range(2):
                xt_far[p, g] = xs_far[p, g].T
            wait_gather(g)

        @pl.loop(2 * (u % 2), 2 * (u % 2) + 2)
        def _(j):
            part_one(g, j)

    def compute_two(u):
        @pl.when(u % 2 == 1)
        def _():
            part_two(u // 2)

    def gather_sent(c):
        for stage in range(4):
            each(lambda a, k: ag_copy(a, c, stage, k).wait_send())
        for a in range(2):
            zh_copy(a, c).wait_send()
            for p in range(2):
                tok_copy(a, p, c).wait_send()

    def scatter_sent(c):
        for stage in range(4):
            each(lambda a, k: rs_copy(a, c, stage, k).wait_send())
        for a in range(2):
            z_copy(a, c).wait_send()

    @pl.loop(0, R + 6)
    def _(u):
        event(u, 0, compute, R)

        @pl.when((u % 2 == 1) & (u < 2 * (C - EARLY)))
        def _():
            ag_next(3)(EARLY + u // 2)

        event(u, 0, rs_start, R)
        event(u, 2, rs_one, R)
        event(u, 0, compute_two, R)
        event(u, 4, rs_three, R)
        event(u, 5, rs_four, R)

        event(u, 3, rs_two, R)

        @pl.when(u == R + 1)
        def _():
            finish()

        event(u, 6, rs_last, R)
        event(u, 6, scatter_sent, R)
        event(u, 4, gather_sent)


def hand_over(*refs):
    n = 4
    ins, outs, bufs, (sem_in, sem_out) = refs[:n], refs[n : 2 * n], refs[2 * n : 3 * n], refs[3 * n :]
    copies = []
    for i in range(n):
        parts = 4 if i < 2 else 1
        rows = ins[i].shape[0] // parts
        for k in range(parts):
            at = pl.ds(k * rows, rows)
            copies.append(
                (
                    pltpu.make_async_copy(ins[i].at[at], bufs[i].at[at], sem_in.at[i, k]),
                    pltpu.make_async_copy(bufs[i].at[at], outs[i].at[at], sem_out.at[i, k]),
                )
            )
    for first, _ in copies:
        first.start()
    for first, second in copies:
        first.wait()
        second.start()
    for _, second in copies:
        second.wait()


def per_device(tokens, out_cot, kept, w_in, w_out):
    vmem = pl.BlockSpec(memory_space=pltpu.VMEM)
    hbm = pl.BlockSpec(memory_space=pl.ANY)
    dma = pltpu.SemaphoreType.DMA
    full = pltpu.VMEM((C, 4, 4, NB, 16, BLK), BF16)
    term = pltpu.VMEM((R, 4, 4, RB, 16, BLK), BF16)
    row = (TOK, BLK)
    results = pl.pallas_call(
        kernel,
        out_shape=(
            jax.ShapeDtypeStruct(tokens.shape, BF16),
            jax.ShapeDtypeStruct(tokens.shape, BF16),
            jax.ShapeDtypeStruct((R, RB, 8, BLK), F32),
            jax.ShapeDtypeStruct((R, RB, 8, BLK), F32),
        ),
        in_specs=[pl.BlockSpec(memory_space=pltpu.SMEM), hbm, hbm, vmem, vmem],
        out_specs=(hbm, hbm, vmem, vmem),
        scratch_shapes=[
            full,
            full,
            term,
            term,
            pltpu.VMEM((2, R, 2, 2, RB, 16, BLK), BF16),
            pltpu.VMEM((2, R, 2, 4, RB, 16, BLK), BF16),
            pltpu.VMEM((2, R, 2, RB // 2, 16, BLK), BF16),
            pltpu.VMEM((2, R, 2, RB, 16, BLK), BF16),
            pltpu.VMEM((2, C * NB * 8, BLK), BF16),
            pltpu.VMEM((2, R, RB * 8, BLK), BF16),
            pltpu.VMEM((2, R, RB * 8, BLK), BF16),
            pltpu.VMEM((C,) + row, BF16),
            pltpu.VMEM((C,) + row, BF16),
            pltpu.VMEM((C, BLK, TOK), BF16),
            pltpu.VMEM((2, C) + row, BF16),
            pltpu.VMEM((2, C) + row, BF16),
            pltpu.VMEM((2, C, BLK, TOK), BF16),
            pltpu.VMEM((C,) + row, F32),
            pltpu.VMEM((C,) + row, F32),
            pltpu.VMEM((2, 2, C) + row, BF16),
            pltpu.VMEM((2, 2, C) + row, BF16),
            pltpu.VMEM((J,) + row, BF16),
            pltpu.VMEM((J,) + row, BF16),
            dma((2, C, 4, 2)),
            dma((2, C, 4, 2)),
            dma((2, R, 4, 2)),
            dma((2, R, 4, 2)),
            dma((2, C)),
            dma((2, C)),
            dma((2, 2, C)),
            dma((2, 2, C)),
            dma((2, 2, C)),
            dma((2, 2, C)),
            dma((2, R)),
            dma((2, R)),
            dma((2, C)),
        ],
        compiler_params=pltpu.CompilerParams(
            collective_id=0, has_side_effects=True, vmem_limit_bytes=64 * 2**20
        ),
        cost_estimate=pl.CostEstimate(
            flops=24 * 10**9, bytes_accessed=8 * 2**20, transcendentals=4 * 2**20
        ),
    )(kept.T, tokens, out_cot, w_in.reshape(C * NB * 8, BLK), w_out.reshape(C * NB * 8, BLK))
    mixed, tokens_grad, w_in_grad, w_out_grad = pl.pallas_call(
        hand_over,
        out_shape=tuple(jax.ShapeDtypeStruct(r.shape, r.dtype) for r in results),
        in_specs=[hbm] * 4,
        out_specs=(hbm,) * 4,
        scratch_shapes=[pltpu.VMEM(r.shape, r.dtype) for r in results] + [dma((4, 4)), dma((4, 4))],
    )(*results)
    shape = w_in.shape
    return mixed, tokens_grad, w_in_grad.reshape(shape), w_out_grad.reshape(shape)


def solution(mesh):
    wide, blocks = P("dp", "tensor"), P("tensor", None, "dp", None)
    return jax.shard_map(
        per_device,
        mesh=mesh,
        in_specs=(wide, wide, P("tensor", None), blocks, blocks),
        out_specs=(wide, wide, blocks, blocks),
        check_vma=False,
    )
```

```python
import functools

import jax
import jax.numpy as jnp
from jax import lax
from jax.experimental import pallas as pl
from jax.experimental.pallas import tpu as pltpu
from jax.sharding import PartitionSpec as P

MESH = pl.DeviceIdType.MESH
F32, BF16 = jnp.float32, jnp.bfloat16
C = 4
J = 4
NB = 12
R = 2 * C
RB = NB // 2
EARLY = 3
BLK = 256
TOK = 512
SIGNS = (1, -1)


def nn(a, b):
    return lax.dot_general(a, b, (((1,), (0,)), ((), ())), preferred_element_type=F32)


def nt(a, b):
    return lax.dot_general(a, b, (((1,), (1,)), ((), ())), preferred_element_type=F32)


def kernel(
    kept,
    tokens,
    out_cot,
    w_in,
    w_out,
    mixed,
    tokens_grad,
    w_in_grad,
    w_out_grad,
    g_in,
    g_out,
    t_in,
    t_out,
    r0,
    r1,
    r2,
    r3,
    zh_recv,
    z_send,
    z_recv,
    xs,
    cs,
    xt,
    xs_far,
    cs_far,
    xt_far,
    acc_m,
    acc_n,
    far_send,
    far_recv,
    act_all,
    pg_all,
    ag_send_sem,
    ag_recv_sem,
    rs_send_sem,
    rs_recv_sem,
    zh_send_sem,
    zh_recv_sem,
    tok_send_sem,
    tok_recv_sem,
    far_send_sem,
    far_recv_sem,
    z_send_sem,
    z_recv_sem,
    local_sem,
):
    dp = lax.axis_index("dp")
    te = lax.axis_index("tensor")
    y, x, zh = dp // 8, (dp // 2) % 4, dp % 2
    scale = float(TOK * 32) ** -0.5

    def at(yy, xx, zz):
        return {"dp": (yy % 4) * 8 + (xx % 4) * 2 + zz}

    def beside(axis, d):
        return at(y, x + d + 4, zh) if axis == 0 else at(y + d + 4, x, zh)

    across = {"dp": dp + 1 - 2 * zh}
    core_peer = {"tensor": te + 1 - 2 * (te % 2)}
    z_peer = {"tensor": (te + 2) % 4}
    peers = (core_peer, z_peer)

    def remote(src, dst, send, recv, to):
        return pltpu.make_async_remote_copy(
            src_ref=src, dst_ref=dst, send_sem=send, recv_sem=recv, device_id=to, device_id_type=MESH
        )

    def load(kind, i):
        src, dst = ((tokens, xs), (out_cot, cs))[kind]
        return pltpu.make_async_copy(
            src.at[:, pl.ds(BLK * i, BLK)], dst.at[i], local_sem.at[kind, i]
        )

    for kind in range(2):
        for i in range(C):
            load(kind, i).start()

    barrier = pltpu.get_barrier_semaphore()
    everyone = [across, core_peer, z_peer] + [beside(a, d) for a in (0, 1) for d in SIGNS]
    for to in everyone:
        pl.semaphore_signal(barrier, inc=1, device_id=to, device_id_type=MESH)
    pl.semaphore_wait(barrier, len(everyone))

    def zh_copy(a, c):
        rows = pl.ds(c * NB * 8, NB * 8)
        return remote(
            (w_in, w_out)[a].at[rows],
            zh_recv.at[a, rows],
            zh_send_sem.at[a, c],
            zh_recv_sem.at[a, c],
            across,
        )

    for c in range(C):
        for a in range(2):
            zh_copy(a, c).start()

    def tok_copy(kind, p, i):
        return remote(
            (xs, cs)[kind].at[i],
            (xs_far, cs_far)[kind].at[p, i],
            tok_send_sem.at[kind, p, i],
            tok_recv_sem.at[kind, p, i],
            peers[p],
        )

    for kind in range(2):
        for i in range(C):
            load(kind, i).wait()

    def join(a, c):
        rows = pl.ds(c * NB * 8, NB * 8)
        own = (w_in, w_out)[a][rows].astype(F32).reshape(NB, 8, BLK)
        got = zh_recv[a, rows].astype(F32).reshape(NB, 8, BLK)
        low = jnp.where(zh == 0, own, got)
        high = jnp.where(zh == 0, got, own)
        (g_in, g_out)[a][c, y, x] = jnp.concatenate([low, high], axis=1).astype(BF16)

    def opposite(v, d):
        return (v - d + 4) % 4

    def half(d, n):
        return pl.ds(0, n // 2) if d == 1 else pl.ds(n // 2, n // 2)

    def ag_copy(a, c, stage, k):
        d = SIGNS[k]
        g = (g_in, g_out)[a].at[c]
        if stage == 0:
            ref, axis = g.at[y, x], a
        elif stage == 1:
            ref = (g.at[y, opposite(x, d)] if a == 0 else g.at[opposite(y, d), x]).at[half(d, NB)]
            axis = a
        elif stage == 2:
            ref, axis = (g.at[y] if a == 0 else g.at[:, x]), 1 - a
        else:
            ref = g.at[opposite(y, d), half(d, 4)] if a == 0 else g.at[half(d, 4), opposite(x, d)]
            axis = 1 - a
        return remote(
            ref, ref, ag_send_sem.at[a, c, stage, k], ag_recv_sem.at[a, c, stage, k], beside(axis, d)
        )

    def each(fn):
        for a in range(2):
            for k in range(2):
                fn(a, k)

    def transpose(i):
        xt[i] = xs[i].T

    def ag_zero(c):
        for a in range(2):
            zh_copy(a, c).wait_recv()
            join(a, c)
            for k in range(2):
                ag_copy(a, c, 0, k).start()
        for kind in range(2):
            for p in range(2):
                tok_copy(kind, p, c).start()

    def ag_next(stage):
        def go(c):
            for a in range(2):
                for k in range(2):
                    ag_copy(a, c, stage - 1, k).wait_recv()
                    if stage != 2:
                        ag_copy(a, c, stage, k).start()
                if stage == 2:
                    for k in range(2):
                        ag_copy(a, c, stage, k).start()

        return go

    def event(t, behind, fn, count=C):
        @pl.when((t >= behind) & (t < count + behind))
        def _():
            fn(t - behind)

    @pl.loop(0, C + 2)
    def _(t):
        event(t, 0, ag_zero)
        event(t, 1, ag_next(1))
        event(t, 2, ag_next(2))
        event(t, 3, ag_next(3), EARLY)
        event(t, 0, transpose)

    acc_m[...] = jnp.zeros_like(acc_m)
    acc_n[...] = jnp.zeros_like(acc_n)

    def rs_copy(a, c, stage, k):
        d = SIGNS[k]
        t = (t_in, t_out)[a].at[c]
        if stage == 0:
            src = t.at[(y + 2) % 4, half(d, 4)] if a == 0 else t.at[half(d, 4), (x + 2) % 4]
            dst, axis = r0, 1 - a
        elif stage == 1:
            src = t.at[(y + d + 4) % 4] if a == 0 else t.at[:, (x + d + 4) % 4]
            dst, axis = r1, 1 - a
        elif stage == 2:
            src = (t.at[y, (x + 2) % 4] if a == 0 else t.at[(y + 2) % 4, x]).at[half(d, RB)]
            dst, axis = r2, a
        else:
            src = t.at[y, (x + d + 4) % 4] if a == 0 else t.at[(y + d + 4) % 4, x]
            dst, axis = r3, a
        return remote(
            src,
            dst.at[a, c, k],
            rs_send_sem.at[a, c, stage, k],
            rs_recv_sem.at[a, c, stage, k],
            beside(axis, d),
        )

    def add(p, q):
        return p.astype(F32) + q.astype(F32)

    def rs_start(c):
        each(lambda a, k: rs_copy(a, c, 0, k).start())

    def rs_one(c):
        def go(a, k):
            d = SIGNS[k]
            rs_copy(a, c, 0, k).wait_recv()
            if a == 0:
                yy = (y + d + 4) % 4
                t_in[c, yy, half(d, 4)] = add(t_in[c, yy, half(d, 4)], r0[a, c, k]).astype(BF16)
            else:
                xx = (x + d + 4) % 4
                t_out[c, half(d, 4), xx] = add(t_out[c, half(d, 4), xx], r0[a, c, k]).astype(BF16)
            rs_copy(a, c, 1, k).start()

        each(go)

    def rs_two(c):
        for a in range(2):
            for k in range(2):
                rs_copy(a, c, 1, k).wait_recv()
            got = add(r1[a, c, 0], r1[a, c, 1])
            if a == 0:
                t_in[c, y] = (t_in[c, y].astype(F32) + got).astype(BF16)
            else:
                t_out[c, :, x] = (t_out[c, :, x].astype(F32) + got).astype(BF16)
            for k in range(2):
                rs_copy(a, c, 2, k).start()

    def rs_three(c):
        def go(a, k):
            d = SIGNS[k]
            rs_copy(a, c, 2, k).wait_recv()
            if a == 0:
                xx = (x + d + 4) % 4
                t_in[c, y, xx, half(d, RB)] = add(t_in[c, y, xx, half(d, RB)], r2[a, c, k]).astype(BF16)
            else:
                yy = (y + d + 4) % 4
                t_out[c, yy, x, half(d, RB)] = add(t_out[c, yy, x, half(d, RB)], r2[a, c, k]).astype(BF16)
            rs_copy(a, c, 3, k).start()

        each(go)

    def z_copy(a, c):
        return remote(
            z_send.at[a, c], z_recv.at[a, c], z_send_sem.at[a, c], z_recv_sem.at[a, c], across
        )

    def rs_four(c):
        for a in range(2):
            for k in range(2):
                rs_copy(a, c, 3, k).wait_recv()
            total = add(r3[a, c, 0], r3[a, c, 1]) + (t_in, t_out)[a][c, y, x].astype(F32)
            low, high = total[:, :8], total[:, 8:]
            mine = jnp.where(zh == 0, low, high)
            other = jnp.where(zh == 0, high, low)
            z_send[a, c] = other.reshape(RB * 8, BLK).astype(BF16)
            (w_in_grad, w_out_grad)[a][c] = mine
            z_copy(a, c).start()

    def rs_last(c):
        for a in range(2):
            z_copy(a, c).wait_recv()
            out = (w_in_grad, w_out_grad)[a]
            out[c] = out[c] + z_recv[a, c].astype(F32).reshape(RB, 8, BLK)

    def choose(near, far, section, g):
        other = jnp.where(section == 0, g + 1 - 2 * (g % 2), (g + 2) % 4)
        return jnp.where(
            section < 2, near[other], jnp.where(section == 2, far[0, g], far[1, g])
        )

    def block(ref, g, b):
        return ref[g, :, :, b].reshape(BLK, BLK)

    def part_one(g, j):
        h = J * g + j
        x_s, c_s, t_s = [
            [near[g]] + [choose(near, far, kept[s, h], g) for s in range(2)]
            for near, far in ((xs, xs_far), (cs, cs_far), (xt, xt_far))
        ]
        ws = [block(g_in, g, 3 * j + s) for s in range(3)]
        pre = nn(x_s[0], ws[0]) + nn(x_s[1], ws[1]) + nn(x_s[2], ws[2])
        cdf = 0.5 * (1.0 + lax.erf(pre * 0.7071067811865476))
        act = (pre * cdf).astype(BF16)
        slope = cdf + pre * jnp.exp(-0.5 * pre * pre) * 0.3989422804014327
        vs = [block(g_out, g, 3 * j + s) for s in range(3)]
        act_grad = nt(c_s[0], vs[0]) + nt(c_s[1], vs[1]) + nt(c_s[2], vs[2])
        pg = (act_grad * slope).astype(BF16)
        act_all[j] = act
        pg_all[j] = pg
        act_t = act.T
        for s in range(3):
            out_term = (nn(act_t, c_s[s]) * scale).astype(BF16)
            t_out[2 * g + j // 2, :, :, 3 * (j % 2) + s] = out_term.reshape(4, 4, 16, BLK)
            in_term = (nn(t_s[s], pg) * scale).astype(BF16)
            t_in[2 * g + j // 2, :, :, 3 * (j % 2) + s] = in_term.reshape(4, 4, 16, BLK)

    def far_copy(kind, p, g):
        return remote(
            far_send.at[kind, p, g],
            far_recv.at[kind, p, g],
            far_send_sem.at[kind, p, g],
            far_recv_sem.at[kind, p, g],
            peers[p],
        )

    def part_two(g):
        def pick(ref, section):
            def one(j):
                h = J * g + j
                parts = []
                for s in range(2):
                    flag = jnp.where(kept[s, h] == section, 1.0, 0.0).astype(F32)
                    parts.append(block(ref, g, 3 * j + 1 + s).astype(F32) * flag)
                return (parts[0] + parts[1]).astype(BF16)

            return [one(j) for j in range(J)]

        def own(ref):
            return [block(ref, g, 3 * j) for j in range(J)]

        def total(kind, ws):
            if kind == 0:
                act = jnp.concatenate([act_all[j] for j in range(J)], axis=1)
                return nn(act, jnp.concatenate(ws, axis=0))
            pg = jnp.concatenate([pg_all[j] for j in range(J)], axis=1)
            return nt(pg, jnp.concatenate(ws, axis=1))

        for kind in range(2):
            ref = (g_out, g_in)[kind]
            acc = (acc_m, acc_n)[kind]
            for p in range(2):
                far_send[kind, p, g] = total(kind, pick(ref, 2 + p)).astype(BF16)
                far_copy(kind, p, g).start()
            acc[g] = acc[g] + total(kind, own(ref))
            near = (g + 1 - 2 * (g % 2), (g + 2) % 4)
            for p in range(2):
                acc[near[p]] = acc[near[p]] + total(kind, pick(ref, p))

    def wait_gather(c):
        each(lambda a, k: ag_copy(a, c, 3, k).wait_recv())

    def finish():
        def out_copy(kind, g):
            stage = (act_all, pg_all)[kind]
            out = (mixed, tokens_grad)[kind]
            return pltpu.make_async_copy(
                stage.at[g], out.at[:, pl.ds(BLK * g, BLK)], local_sem.at[kind, g]
            )

        for kind in range(2):
            for g in range(C):
                for p in range(2):
                    far_copy(kind, p, g).wait_recv()
                    far_copy(kind, p, g).wait_send()
                value = (acc_m, acc_n)[kind][g] + add(far_recv[kind, 0, g], far_recv[kind, 1, g])
                (act_all, pg_all)[kind][g] = value.astype(BF16)
                out_copy(kind, g).start()
        for kind in range(2):
            for g in range(C):
                out_copy(kind, g).wait()

    def compute(u):
        g = u // 2

        @pl.when(u % 2 == 0)
        def _():
            for kind in range(2):
                for p in range(2):
                    tok_copy(kind, p, g).wait_recv()
            for p in range(2):
                xt_far[p, g] = xs_far[p, g].T
            wait_gather(g)

        @pl.loop(2 * (u % 2), 2 * (u % 2) + 2)
        def _(j):
            part_one(g, j)

    def compute_two(u):
        @pl.when(u % 2 == 1)
        def _():
            part_two(u // 2)

    def gather_sent(c):
        for stage in range(4):
            each(lambda a, k: ag_copy(a, c, stage, k).wait_send())
        for a in range(2):
            zh_copy(a, c).wait_send()
            for p in range(2):
                tok_copy(a, p, c).wait_send()

    def scatter_sent(c):
        for stage in range(4):
            each(lambda a, k: rs_copy(a, c, stage, k).wait_send())
        for a in range(2):
            z_copy(a, c).wait_send()

    @pl.loop(0, R + 6)
    def _(u):
        event(u, 0, compute, R)

        @pl.when((u % 2 == 1) & (u < 2 * (C - EARLY)))
        def _():
            ag_next(3)(EARLY + u // 2)

        event(u, 0, rs_start, R)
        event(u, 2, rs_one, R)
        event(u, 0, compute_two, R)
        event(u, 3, rs_two, R)
        event(u, 4, rs_three, R)
        event(u, 5, rs_four, R)


        @pl.when(u == R + 1)
        def _():
            finish()

        event(u, 6, rs_last, R)
        event(u, 6, scatter_sent, R)
        event(u, 4, gather_sent)


def hand_over(*refs):
    n = 4
    ins, outs, bufs, (sem_in, sem_out) = refs[:n], refs[n : 2 * n], refs[2 * n : 3 * n], refs[3 * n :]
    copies = []
    for i in range(n):
        parts = 4 if i < 2 else 1
        rows = ins[i].shape[0] // parts
        for k in range(parts):
            at = pl.ds(k * rows, rows)
            copies.append(
                (
                    pltpu.make_async_copy(ins[i].at[at], bufs[i].at[at], sem_in.at[i, k]),
                    pltpu.make_async_copy(bufs[i].at[at], outs[i].at[at], sem_out.at[i, k]),
                )
            )
    for first, _ in copies:
        first.start()
    for first, second in copies:
        first.wait()
        second.start()
    for _, second in copies:
        second.wait()


def per_device(tokens, out_cot, kept, w_in, w_out):
    vmem = pl.BlockSpec(memory_space=pltpu.VMEM)
    hbm = pl.BlockSpec(memory_space=pl.ANY)
    dma = pltpu.SemaphoreType.DMA
    full = pltpu.VMEM((C, 4, 4, NB, 16, BLK), BF16)
    term = pltpu.VMEM((R, 4, 4, RB, 16, BLK), BF16)
    row = (TOK, BLK)
    results = pl.pallas_call(
        kernel,
        out_shape=(
            jax.ShapeDtypeStruct(tokens.shape, BF16),
            jax.ShapeDtypeStruct(tokens.shape, BF16),
            jax.ShapeDtypeStruct((R, RB, 8, BLK), F32),
            jax.ShapeDtypeStruct((R, RB, 8, BLK), F32),
        ),
        in_specs=[pl.BlockSpec(memory_space=pltpu.SMEM), hbm, hbm, vmem, vmem],
        out_specs=(hbm, hbm, vmem, vmem),
        scratch_shapes=[
            full,
            full,
            term,
            term,
            pltpu.VMEM((2, R, 2, 2, RB, 16, BLK), BF16),
            pltpu.VMEM((2, R, 2, 4, RB, 16, BLK), BF16),
            pltpu.VMEM((2, R, 2, RB // 2, 16, BLK), BF16),
            pltpu.VMEM((2, R, 2, RB, 16, BLK), BF16),
            pltpu.VMEM((2, C * NB * 8, BLK), BF16),
            pltpu.VMEM((2, R, RB * 8, BLK), BF16),
            pltpu.VMEM((2, R, RB * 8, BLK), BF16),
            pltpu.VMEM((C,) + row, BF16),
            pltpu.VMEM((C,) + row, BF16),
            pltpu.VMEM((C, BLK, TOK), BF16),
            pltpu.VMEM((2, C) + row, BF16),
            pltpu.VMEM((2, C) + row, BF16),
            pltpu.VMEM((2, C, BLK, TOK), BF16),
            pltpu.VMEM((C,) + row, F32),
            pltpu.VMEM((C,) + row, F32),
            pltpu.VMEM((2, 2, C) + row, BF16),
            pltpu.VMEM((2, 2, C) + row, BF16),
            pltpu.VMEM((J,) + row, BF16),
            pltpu.VMEM((J,) + row, BF16),
            dma((2, C, 4, 2)),
            dma((2, C, 4, 2)),
            dma((2, R, 4, 2)),
            dma((2, R, 4, 2)),
            dma((2, C)),
            dma((2, C)),
            dma((2, 2, C)),
            dma((2, 2, C)),
            dma((2, 2, C)),
            dma((2, 2, C)),
            dma((2, R)),
            dma((2, R)),
            dma((2, C)),
        ],
        compiler_params=pltpu.CompilerParams(
            collective_id=0, has_side_effects=True, vmem_limit_bytes=64 * 2**20
        ),
        cost_estimate=pl.CostEstimate(
            flops=24 * 10**9, bytes_accessed=8 * 2**20, transcendentals=4 * 2**20
        ),
    )(kept.T, tokens, out_cot, w_in.reshape(C * NB * 8, BLK), w_out.reshape(C * NB * 8, BLK))
    mixed, tokens_grad, w_in_grad, w_out_grad = pl.pallas_call(
        hand_over,
        out_shape=tuple(jax.ShapeDtypeStruct(r.shape, r.dtype) for r in results),
        in_specs=[hbm] * 4,
        out_specs=(hbm,) * 4,
        scratch_shapes=[pltpu.VMEM(r.shape, r.dtype) for r in results] + [dma((4, 4)), dma((4, 4))],
    )(*results)
    shape = w_in.shape
    return mixed, tokens_grad, w_in_grad.reshape(shape), w_out_grad.reshape(shape)


def solution(mesh):
    wide, blocks = P("dp", "tensor"), P("tensor", None, "dp", None)
    return jax.shard_map(
        per_device,
        mesh=mesh,
        in_specs=(wide, wide, P("tensor", None), blocks, blocks),
        out_specs=(wide, wide, blocks, blocks),
        check_vma=False,
    )
```
